32 devices in a mesh: ser: 8 (over z, y), org: 4 (over x, core).
Axes of the slice: x: 2, y: 2, z: 4, core: 2. Of those that a mesh axis runs over, the one named last changes fastest.
Arguments:
- residual: float32 [64, 8192], P('org', 'ser'), may hold values from -48 to 48
- sub_size: int32 [16], replicated, may hold values from 256 to 1280, as said below
- sub_owner: int32 [16], replicated, may hold values from 0 to 7, as said below
- series_perm: int32 [8192], replicated, may hold values from 0 to 8191, as said below
Outputs:
- whitened: float32 [64, 8192], P('org', 'ser')
- log_diag: float32 [8, 2048], P('ser', 'org')
The draws below stay inside these ranges and needn't reach their ends.
Inputs may be any that keep to these rules, and one draw needn't show every extreme that they name: `sub_size`: every size is a multiple of 256; the sizes sum to 8192. `sub_owner`: the subtrees of one owner hold at most 2048 series together; some owner holds exactly 2048. `series_perm`: A permutation of the series. Of the 1024 series of one index of ser, at most 256 lie in subtrees of any one owner; some owner receives exactly 256 from every index.
All inputs are finite; a program needn't handle non-finite values.
Results may differ from the reference program's by a relative error of at most 0.0003.
Values sent between devices are 32-bit elements; how exact they have to be, the bound alone decides.
No kernel may reach another device: no remote copies, remote signals or barrier semaphores. Data moves between devices by JAX's collectives and lax.ppermute only.
A program may use at most 192 MiB of HBM per device.

```python
import jax
import jax.numpy as jnp
from jax import lax

SLOTS = 2048
TILE = 256
SER_DEV = 1024
SERIES = 8192
ORIG = 64
N_SER = 8


def layout_draw(key):
    tiles = SLOTS // TILE
    pairs = N_SER // 2
    sub_keys = jax.random.split(key, 5)
    cut_keys = jax.random.split(sub_keys[0], pairs)

    def cut_set(one_key):
        chosen = jax.random.permutation(one_key, tiles - 1)[:3] + 1
        return jnp.sort(chosen).astype(jnp.int32)
    cut_points = jax.vmap(cut_set)(cut_keys)
    full_pair = jax.random.randint(sub_keys[1], (), 0, pairs)
    is_full = (jnp.arange(pairs) == full_pair)[:, None]
    cut_points = jnp.where(is_full, jnp.arange(1, 4, dtype=jnp.int32)[None, :], cut_points)
    bounds = jnp.concatenate([jnp.zeros((pairs, 1), jnp.int32), cut_points, jnp.full((pairs, 1), tiles, jnp.int32)], axis=1)
    sub_size = ((bounds[:, 1:] - bounds[:, :-1]) * TILE).reshape(-1).astype(jnp.int32)
    owner_bit = jax.random.randint(sub_keys[2], (pairs, 4), 0, 2)
    owner_bit = jnp.where(is_full, 0, owner_bit)
    sub_owner = (2 * jnp.arange(pairs, dtype=jnp.int32)[:, None] + owner_bit).reshape(-1).astype(jnp.int32)
    subtree_count = sub_size.shape[0]
    owner_ids = jnp.arange(N_SER, dtype=jnp.int32)
    loads = jnp.sum(jnp.where(sub_owner[None, :] == owner_ids[:, None], sub_size[None, :], 0), axis=1).astype(jnp.int32)
    offset_ser = jax.random.randint(sub_keys[3], (N_SER,), 0, N_SER)
    per_source = loads // N_SER
    prior_count = (jnp.cumsum(per_source) - per_source).astype(jnp.int32)
    slot_ids = jnp.arange(SLOTS, dtype=jnp.int32)
    source_of = (slot_ids[None, :] + offset_ser[:, None]) % N_SER
    rank_in = prior_count[:, None] + slot_ids[None, :] // N_SER
    rank_in = jnp.minimum(rank_in, SER_DEV - 1)
    shuffle_keys = jax.random.split(sub_keys[4], N_SER)
    shuffle = jax.vmap(lambda one_key: jax.random.permutation(one_key, SER_DEV))(shuffle_keys).astype(jnp.int32)
    series_of_slot = source_of * SER_DEV + shuffle.reshape(-1)[source_of * SER_DEV + rank_in]
    end_pos = jnp.cumsum(sub_size).astype(jnp.int32)
    start_pos = end_pos - sub_size
    order_ids = jnp.arange(subtree_count, dtype=jnp.int32)
    earlier = (sub_owner[None, :] == sub_owner[:, None]) & (order_ids[None, :] < order_ids[:, None])
    slot_start = jnp.sum(jnp.where(earlier, sub_size[None, :], 0), axis=1).astype(jnp.int32)
    position = jnp.arange(SERIES, dtype=jnp.int32)
    subtree_of = jnp.sum((position[:, None] >= end_pos[None, :]).astype(jnp.int32), axis=1).astype(jnp.int32)
    slot_here = slot_start[subtree_of] + position - start_pos[subtree_of]
    series_perm = series_of_slot.reshape(-1)[sub_owner[subtree_of] * SLOTS + slot_here].astype(jnp.int32)
    return (sub_size, sub_owner, series_perm, subtree_of)


def draw_sub_size(key, part):
    return layout_draw(key)[0]


def draw_sub_owner(key, part):
    return layout_draw(key)[1]


def draw_series_perm(key, part):
    return layout_draw(key)[2]


def draw_residual(key, part):
    layout = layout_draw(key)
    series_perm = layout[2]
    subtree_of = layout[3]
    key = jax.random.fold_in(key, 7)
    sub_keys = jax.random.split(key, 5)
    subtree_count = 2 * N_SER
    tree_of_series = jnp.zeros((SERIES,), jnp.int32).at[series_perm].set(subtree_of)
    pick = jax.random.uniform(sub_keys[0], (subtree_count,))
    loading = jnp.where(pick < 0.25, 0.0, 0.176 * jnp.sqrt(jax.random.uniform(sub_keys[1], (subtree_count,))))
    factor = jnp.clip(jax.random.normal(sub_keys[2], (ORIG, subtree_count)), -4.0, 4.0)
    noise = jnp.clip(jax.random.normal(sub_keys[3], (ORIG, SERIES)), -4.0, 4.0)
    scale = jnp.exp(jax.random.uniform(sub_keys[4], (SERIES,), minval=0.0, maxval=2.302585))
    common = jnp.take(factor, tree_of_series, axis=1) * jnp.take(loading, tree_of_series)[None, :]
    return (scale[None, :] * (common + noise)).astype(jnp.float32)


def setup_inputs(seed: int = 0) -> dict:
    key_list = jax.random.split(jax.random.key(seed), 5)
    residual = draw_residual(jax.random.fold_in(key_list[4], 71), 0)
    sub_size = draw_sub_size(jax.random.fold_in(key_list[4], 71), 0)
    sub_owner = draw_sub_owner(jax.random.fold_in(key_list[4], 71), 0)
    series_perm = draw_series_perm(jax.random.fold_in(key_list[4], 71), 0)
    return dict(residual=residual, sub_size=sub_size, sub_owner=sub_owner, series_perm=series_perm)


epsilon = 1e-06

def slot_tables(sub_size, sub_owner, series_perm, owner_count, slot_count):
    subtree_count = sub_size.shape[0]
    series_count = series_perm.shape[0]
    end_pos = jnp.cumsum(sub_size).astype(jnp.int32)
    start_pos = (end_pos - sub_size).astype(jnp.int32)
    order_ids = jnp.arange(subtree_count, dtype=jnp.int32)
    earlier = (sub_owner[None, :] == sub_owner[:, None]) & (order_ids[None, :] < order_ids[:, None])
    slot_start = lax.optimization_barrier(jnp.sum(jnp.where(earlier, sub_size[None, :], 0), axis=1)).astype(jnp.int32)
    position = jnp.arange(series_count, dtype=jnp.int32)
    subtree_of = lax.optimization_barrier(jnp.sum((position[:, None] >= end_pos[None, :]).astype(jnp.int32), axis=1)).astype(jnp.int32)
    placed = (sub_owner[subtree_of] * slot_count + slot_start[subtree_of] + position - start_pos[subtree_of]).astype(jnp.int32)
    empty_table = jnp.full((owner_count * slot_count,), -1, jnp.int32)
    slot_series = empty_table.at[placed].set(series_perm.astype(jnp.int32))
    slot_subtree = empty_table.at[placed].set(subtree_of)
    return (slot_series.reshape(owner_count, slot_count), slot_subtree.reshape(owner_count, slot_count))

def gram_pair(block):
    highest = lax.Precision.HIGHEST
    dims = (((0,), (0,)), ((), ()))
    gram_sum = lax.dot_general(block.astype(jnp.float32), block.astype(jnp.float32), dims, precision=highest, preferred_element_type=jnp.float32)
    squared = block * block
    square_gram = lax.dot_general(squared.astype(jnp.float32), squared.astype(jnp.float32), dims, precision=highest, preferred_element_type=jnp.float32)
    return (gram_sum, square_gram)

def shrink_factor(gram_sum, square_gram, anchors, slot_subtree, subtree_count):
    highest = lax.Precision.HIGHEST
    filled = slot_subtree >= 0
    spread = jnp.diagonal(gram_sum) / anchors
    inv_scale = jnp.where(filled, lax.rsqrt(spread + epsilon), 0.0)
    correl = gram_sum / anchors * inv_scale[:, None] * inv_scale[None, :]
    inv_square = inv_scale * inv_scale
    variance = (square_gram / anchors * inv_square[:, None] * inv_square[None, :] - correl * correl) / (anchors - 1)
    slot_total = slot_subtree.shape[0]
    same_tree = (slot_subtree[:, None] == slot_subtree[None, :]) & filled[:, None] & jnp.logical_not(jnp.eye(slot_total, dtype=bool))
    upper_sum = lax.optimization_barrier(jnp.sum(jnp.where(same_tree, variance, 0.0), axis=1))
    lower_sum = lax.optimization_barrier(jnp.sum(jnp.where(same_tree, correl * correl, 0.0), axis=1))
    member = (slot_subtree[:, None] == jnp.arange(subtree_count, dtype=jnp.int32)[None, :]).astype(gram_sum.dtype)
    upper_tree = jnp.dot(upper_sum, member, precision=highest)
    lower_tree = jnp.dot(lower_sum, member, precision=highest)
    upper_slot = jnp.dot(member, upper_tree, precision=highest)
    lower_slot = jnp.dot(member, lower_tree, precision=highest)
    shrink = jnp.minimum(upper_slot / jnp.where(filled, lower_slot, 1.0), 1.0)
    weight = jnp.where(same_tree, (1.0 - shrink)[:, None] * (gram_sum / anchors), 0.0)
    weight = weight + jnp.diag(jnp.where(filled, spread, 1.0))
    return jnp.linalg.cholesky(weight)

def reference(residual, sub_size, sub_owner, series_perm):
    anchors, series_count = residual.shape
    subtree_count = sub_size.shape[0]
    slot_series, slot_subtree = slot_tables(sub_size, sub_owner, series_perm, N_SER, SLOTS)
    padded = jnp.concatenate([residual, jnp.zeros((anchors, 1), residual.dtype)], axis=1)
    columns = jnp.where(slot_series >= 0, slot_series, series_count).astype(jnp.int32)

    def per_owner(operands):
        owner_columns, owner_subtree = operands
        block = jnp.take(padded, owner_columns, axis=1)
        gram_sum, square_gram = gram_pair(block)
        lower = shrink_factor(gram_sum, square_gram, anchors, owner_subtree, subtree_count)
        whitened_slots = lax.linalg.triangular_solve(lower, block, left_side=False, lower=True, transpose_a=True)
        return (whitened_slots, jnp.log(jnp.diagonal(lower)))
    whitened_all, log_diag = lax.map(per_owner, (columns, slot_subtree))
    flat = jnp.moveaxis(whitened_all, 0, 1).reshape(anchors, -1)
    output = jnp.zeros((anchors, series_count + 1), residual.dtype).at[:, columns.reshape(-1)].set(flat)
    return (output[:, :series_count], log_diag)
```

```python
import functools

import jax
import jax.numpy as jnp
from jax import lax
from jax.experimental import pallas as pl
from jax.experimental.pallas import tpu as pltpu
from jax.sharding import PartitionSpec as P

SLOTS = 2048
TILE = 256
LANES = 128
ROWS = TILE // LANES
BLOCK = 64
OWNER_TILES = SLOTS // TILE

epsilon = 1e-06

NN = (((1,), (0,)), ((), ()))
NT = (((1,), (1,)), ((), ()))


def dot_bf16(left, right, dims=NN):
    return lax.dot_general(left, right, dims, preferred_element_type=jnp.float32)


def dot_f32(left, right, dims=NN):
    return lax.dot_general(
        left, right, dims, precision=lax.Precision.HIGHEST, preferred_element_type=jnp.float32
    )


def as_bf16(mask):
    return jnp.where(mask, 1.0, 0.0).astype(jnp.bfloat16)


def split_three(value):
    high = value.astype(jnp.bfloat16)
    rest = value - high.astype(jnp.float32)
    middle = rest.astype(jnp.bfloat16)
    low = (rest - middle.astype(jnp.float32)).astype(jnp.bfloat16)
    return jnp.concatenate([high, middle, low], axis=0)


def join_three(value):
    rows = value.shape[0] // 3
    return value[:rows] + value[rows : 2 * rows] + value[2 * rows :]


def iota(shape, dim):
    return lax.broadcasted_iota(jnp.int32, shape, dim)


def before_in_row(width):
    return as_bf16(iota((LANES, width), 0) < iota((LANES, width), 1))


def pack_body(
    size_ref, owner_ref, x_ref, perm_ref, send_ref, dest_ref, place_ref, *, n_ser, n_org
):
    here = lax.axis_index("ser")
    n_sub = size_ref.shape[0]
    rows = perm_ref.shape[0]
    t_dev, ser_dev = x_ref.shape
    per_peer = SLOTS // n_ser
    shift = ser_dev.bit_length() - 1
    groups = ser_dev // LANES

    def owner_of(row_ids):
        owner = jnp.zeros(row_ids.shape, jnp.int32)
        start = jnp.int32(0)
        for k in range(n_sub):
            owner = jnp.where(row_ids >= start, owner_ref[k], owner)
            start = start + (size_ref[k] >> 7)
        return owner

    owner_down = owner_of(iota((rows, LANES), 0))
    owner_across = owner_of(iota((1, rows), 1))
    down_wide = owner_down[:, :rows] if rows <= LANES else owner_of(iota((rows, rows), 0))
    earlier = as_bf16(
        (down_wide == owner_across) & (iota((rows, rows), 1) < iota((rows, rows), 0))
    )
    mine = as_bf16((perm_ref[...] >> shift) == here)
    in_row = dot_bf16(mine, before_in_row(LANES))
    ahead = dot_bf16(earlier, mine).astype(jnp.bfloat16)
    in_rows = dot_bf16(ahead, jnp.ones((LANES, LANES), jnp.bfloat16))
    place_ref[...] = owner_down * per_peer + (in_row + in_rows).astype(jnp.int32)

    def to_local(g, total):
        at = pl.ds(pl.multiple_of(g * 8, 8), 8)
        series = perm_ref[at, :]
        place = place_ref[at, :]
        local = series & (ser_dev - 1)
        group = jnp.where((series >> shift) == here, local >> 7, -1)
        lane = local & (LANES - 1)
        upper = (place >> 4).astype(jnp.float32)
        lower = (place & 15).astype(jnp.float32)
        lefts, rights = [], []
        for s in range(8):
            hit = iota((groups, LANES), 0) == group[s : s + 1]
            lefts.append(
                jnp.concatenate(
                    [jnp.where(hit, upper[s : s + 1], 0.0), jnp.where(hit, lower[s : s + 1], 0.0)],
                    axis=0,
                ).astype(jnp.bfloat16)
            )
            rights.append(as_bf16(iota((LANES, LANES), 0) == lane[s : s + 1]))
        return total + dot_bf16(
            jnp.concatenate(lefts, axis=1), jnp.concatenate(rights, axis=1), NT
        )

    found = lax.fori_loop(0, rows // 8, to_local, jnp.zeros((2 * groups, LANES), jnp.float32))
    dest = (found[:groups] * 16.0 + found[groups:]).astype(jnp.int32)
    dest_ref[...] = dest
    terms = split_three(x_ref[...])

    def pack(o, carry):
        target = iota((per_peer, LANES), 0) + o * per_peer
        pick = jnp.concatenate([as_bf16(target == dest[h : h + 1]) for h in range(groups)], axis=1)
        columns = join_three(dot_bf16(terms, pick, NT))
        for r in range(n_org):
            send_ref[o * n_org + r] = columns
        return carry

    lax.fori_loop(0, n_ser, pack, 0)


def lane_pick(value, index):
    return jnp.take_along_axis(value, index, axis=1, mode="promise_in_bounds")


def eliminate(parts, size, whole):
    lane = iota((8, LANES), 1)
    sub = iota((8, LANES), 0)
    shift = lane & (LANES - size)
    parts = [list(part) for part in parts]
    downs = [[jnp.ones((8, LANES), jnp.float32)] * len(part) for part in parts]
    acrosses = [jnp.ones((8, LANES), jnp.float32) for _ in parts]
    for j in range(0, size, 2):
        g, s = divmod(j, 8)
        column0 = shift + j
        column1 = shift + (j + 1)
        on0, on1 = lane == column0, lane == column1
        on = on0 | on1
        for p, part in enumerate(parts):
            row0 = jnp.broadcast_to(part[g][s : s + 1], (8, LANES))
            row1 = jnp.broadcast_to(part[g][s + 1 : s + 2], (8, LANES))
            first = lane_pick(row0, column0)
            cross = lane_pick(row0, column1)
            second = lane_pick(row1, column1)
            row0 = jnp.where(on, jnp.where(on0, 1.0, 0.0), row0)
            row1 = jnp.where(on, jnp.where(on1, 1.0, 0.0), row1)
            inv = 1.0 / first
            step = cross * inv
            pivot = second - step * cross
            inv1 = 1.0 / pivot
            next1 = row1 - step * row0
            solved1 = next1 * inv1
            solved0 = row0 * inv - step * solved1
            for i in range(0 if whole else g, len(part)):
                old = part[i]
                new = (
                    jnp.where(on, 0.0, old)
                    - lane_pick(old, column0) * solved0
                    - lane_pick(old, column1) * solved1
                )
                if i == g:
                    if whole:
                        new = jnp.where(sub == s, solved0, jnp.where(sub == s + 1, solved1, new))
                    else:
                        new = jnp.where(sub <= s, old, jnp.where(sub == s + 1, next1, new))
                        new = jnp.where(sub == s, row0, new)
                part[i] = new
            if not whole:
                downs[p][g] = jnp.where(
                    sub == s, first, jnp.where(sub == s + 1, pivot, downs[p][g])
                )
                acrosses[p] = jnp.where(on0, first, jnp.where(on1, pivot, acrosses[p]))
    return parts, downs, acrosses


def owner_body(
    size_ref,
    owner_ref,
    recv_ref,
    perm_ref,
    back_ref,
    log_ref,
    all_ref,
    index_ref,
    pick_ref,
    inverse_ref,
    tile_ref,
    *,
    n_ser,
    n_org,
    ser_dev,
):
    here = lax.axis_index("ser")
    part = lax.axis_index("org")
    n_sub = size_ref.shape[0]
    t_dev = recv_ref.shape[1]
    anchors = t_dev * n_org
    per_peer = SLOTS // n_ser
    share = SLOTS // n_org
    tiles = share // TILE
    shift = ser_dev.bit_length() - 1
    slot_rows = SLOTS // LANES
    wide = max(per_peer, LANES)

    for t in range(OWNER_TILES):
        tile_ref[0, t] = jnp.int32(-1)
        tile_ref[1, t] = jnp.int32(0)
        tile_ref[2, t] = jnp.int32(0)
    at = jnp.int32(0)
    first = jnp.int32(0)
    for k in range(n_sub):
        count = size_ref[k] >> 8
        held = jnp.where(owner_ref[k] == here, count, 0)

        def put(i, carry, at=at, first=first, held=held):
            tile_ref[0, at + i] = first + i
            tile_ref[1, at + i] = at
            tile_ref[2, at + i] = at + held
            return carry

        lax.fori_loop(0, held, put, 0)
        at = at + held
        first = first + count

    for d in range(n_ser):
        for r in range(n_org):
            all_ref[r * t_dev : (r + 1) * t_dev, d * per_peer : (d + 1) * per_peer] = recv_ref[
                d * n_org + r
            ]

    pieces = []
    for t in range(OWNER_TILES):
        place = tile_ref[0, t]
        rows = perm_ref[pl.ds(jnp.maximum(place, 0) * ROWS, ROWS), :]
        pieces.append(jnp.where(place >= 0, rows, -1))
    source = jnp.concatenate(pieces, axis=0) >> shift
    from_peer = jnp.concatenate([as_bf16(source == d) for d in range(n_ser)], axis=0)
    in_row = dot_bf16(from_peer, before_in_row(LANES))
    row_total = dot_bf16(from_peer, jnp.ones((LANES, wide), jnp.bfloat16)).astype(jnp.bfloat16)
    span = n_ser * slot_rows
    left, right = iota((span, span), 0), iota((span, span), 1)
    ahead = as_bf16((left // slot_rows == right // slot_rows) & (right < left))
    base = dot_bf16(ahead, row_total)[:, :LANES]
    rank = jnp.zeros((slot_rows, LANES), jnp.float32)
    for d in range(n_ser):
        rows = slice(d * slot_rows, (d + 1) * slot_rows)
        rank = jnp.where(source == d, in_row[rows] + base[rows], rank)
    index_ref[...] = jnp.where(source >= 0, source * per_peer + rank.astype(jnp.int32), -1)
    left, right = iota((OWNER_TILES * n_ser, span), 0), iota((OWNER_TILES * n_ser, span), 1)
    through = as_bf16(
        (left % n_ser == right // slot_rows)
        & (right % slot_rows < ROWS * (left // n_ser) + ROWS)
    )
    ends = dot_bf16(through, row_total).astype(jnp.int32)[:, :per_peer]
    tile_of = jnp.zeros((n_ser, per_peer), jnp.int32)
    for t in range(OWNER_TILES):
        tile_of += (iota((n_ser, per_peer), 1) >= ends[t * n_ser : (t + 1) * n_ser]).astype(
            jnp.int32
        )
    tile_of = jnp.concatenate([tile_of[d : d + 1] for d in range(n_ser)], axis=1)

    block = all_ref[...]
    spread = jnp.sum(block * block, axis=0, keepdims=True) * (1.0 / anchors)
    scaled = block * jnp.where(spread > 0, lax.rsqrt(spread), 0.0)
    own = spread / (spread + epsilon)
    fourth = jnp.sum(jnp.square(scaled * scaled), axis=0, keepdims=True) * (1.0 / anchors)
    in_tree, ahead_of, filled = [], [], []
    for u in range(tiles):
        t = part * tiles + u
        low, high = tile_ref[1, t], tile_ref[2, t]
        filled.append(tile_ref[0, t] >= 0)
        in_tree.append((tile_of >= low) & (tile_of < high))
        ahead_of.append((tile_of >= low) & (tile_of < t))
    grams = dot_f32(
        jnp.concatenate(
            [scaled * jnp.where(mask, own, 0.0) for mask in in_tree]
            + [jnp.where(mask, scaled, 0.0) for mask in ahead_of],
            axis=0,
        ),
        scaled,
        NT,
    )
    unit = iota((anchors, anchors), 0) == iota((anchors, anchors), 1)
    shrink = []
    for u in range(tiles):
        dual = grams[u * anchors : (u + 1) * anchors] * (1.0 / anchors)
        own_square = jnp.where(in_tree[u], own * own, 0.0)
        square = dual * dual
        total = lambda value: jnp.sum(
            jnp.sum(value, axis=0, keepdims=True), axis=1, keepdims=True
        )
        lower = total(square) - total(own_square)
        upper = total(jnp.where(unit, square, 0.0)) * anchors - total(own_square * fourth)
        upper = (upper - lower) / (anchors - 1)
        shrink.append(jnp.where(filled[u], jnp.minimum(upper / jnp.where(filled[u], lower, 1.0), 1.0), 1.0))

    for i in range(share // LANES):
        row = index_ref[pl.ds(part * (tiles * ROWS) + i, 1), :]
        pick_ref[:, i * LANES : (i + 1) * LANES] = as_bf16(iota((SLOTS, LANES), 0) == row)
    mine = join_three(dot_bf16(split_three(block), pick_ref[...]))
    my_spread = jnp.sum(mine * mine, axis=0, keepdims=True) * (1.0 / anchors)
    mine = mine * jnp.where(my_spread > 0, lax.rsqrt(my_spread), 0.0)
    mine_down = mine.T

    per_tile = TILE // BLOCK
    blocks = share // BLOCK
    side = LANES // anchors
    rows_of = lambda b: slice(b * BLOCK, (b + 1) * BLOCK)
    for u in range(tiles):
        prior = grams[(tiles + u) * anchors : (tiles + u + 1) * anchors]
        gain = (1.0 - shrink[u]) * (1.0 / anchors)
        for v in range(per_tile):
            b = u * per_tile + v
            inverse_ref[b // side, :, (b % side) * anchors : (b % side + 1) * anchors] = (
                jnp.where(unit, shrink[u], 0.0) + gain * prior
            )
            if v < per_tile - 1:
                piece = mine[:, rows_of(b)]
                prior = prior + dot_f32(piece, piece, NT)

    inverses, _, _ = eliminate(
        [
            [inverse_ref[p, i * 8 : (i + 1) * 8, :] for i in range(anchors // 8)]
            for p in range(blocks // side)
        ],
        anchors,
        whole=True,
    )
    inverses = [jnp.concatenate(rows, axis=0) for rows in inverses]

    diagonal = iota((BLOCK, BLOCK), 0) == iota((BLOCK, BLOCK), 1)
    solved, weights = [], []
    for b in range(blocks):
        gain = (1.0 - shrink[b // per_tile]) * (1.0 / anchors)
        inverse = inverses[b // side][:, (b % side) * anchors : (b % side + 1) * anchors]
        solved.append(dot_f32(inverse, mine[:, rows_of(b)]))
        weights.append(
            jnp.where(diagonal, 1.0, 0.0) + gain * dot_f32(mine_down[rows_of(b)], solved[b])
        )
    pairs = [jnp.concatenate(weights[b : b + 2], axis=1) for b in range(0, blocks, 2)]
    lowers, downs, acrosses = eliminate(
        [[pair[i * 8 : (i + 1) * 8] for i in range(BLOCK // 8)] for pair in pairs],
        BLOCK,
        whole=False,
    )
    keep = iota((BLOCK, LANES), 0) >= (iota((BLOCK, LANES), 1) & (BLOCK - 1))
    done, logs = [], []
    for p in range(blocks // 2):
        lower = jnp.concatenate(
            [row * lax.rsqrt(pivot) for row, pivot in zip(lowers[p], downs[p])], axis=0
        )
        lower = jnp.where(keep, lower, 0.0)
        for h in range(2):
            b = 2 * p + h
            u = b // per_tile
            half = slice(h * BLOCK, (h + 1) * BLOCK)
            done.append(dot_f32(solved[b], lower[:, half], NT) * jnp.sqrt(shrink[u]))
            level = acrosses[p][:1, half] * my_spread[:, rows_of(b)] * shrink[u]
            logs.append(jnp.where(filled[u], 0.5 * jnp.log(level), 0.0))
    log_ref[...] = jnp.concatenate(logs, axis=1)
    terms = split_three(jnp.concatenate(done, axis=1))

    for d in range(n_ser):
        columns = join_three(
            dot_bf16(terms, pick_ref[d * per_peer : (d + 1) * per_peer, :], NT)
        )
        for r in range(n_org):
            back_ref[d * n_org + r] = columns[r * t_dev : (r + 1) * t_dev]


def home_body(back_ref, dest_ref, out_ref, *, n_ser, n_org):
    per_peer = back_ref.shape[2]
    pieces = []
    for o in range(n_ser):
        piece = back_ref[o * n_org]
        for q in range(1, n_org):
            piece = piece + back_ref[o * n_org + q]
        pieces.append(piece)
    terms = split_three(jnp.concatenate(pieces, axis=1))
    groups = dest_ref.shape[0]
    step = 2
    for h in range(0, groups, step):
        pick = jnp.concatenate(
            [
                as_bf16(iota((SLOTS, LANES), 0) == dest_ref[h + i : h + i + 1, :])
                for i in range(step)
            ],
            axis=1,
        )
        out_ref[:, h * LANES : (h + step) * LANES] = join_three(dot_bf16(terms, pick))


def per_device(residual, sub_size, sub_owner, series_perm):
    n_ser = lax.axis_size("ser")
    n_org = lax.axis_size("org")
    t_dev, ser_dev = residual.shape
    anchors = t_dev * n_org
    per_peer = SLOTS // n_ser
    share = SLOTS // n_org
    blocks = share // BLOCK
    side = LANES // anchors
    perm = series_perm.reshape(-1, LANES)
    vmem = pl.BlockSpec(memory_space=pltpu.VMEM)
    smem = pl.BlockSpec(memory_space=pltpu.SMEM)
    params = pltpu.CompilerParams(vmem_limit_bytes=48 * 1024 * 1024)
    blocks_shape = jax.ShapeDtypeStruct((n_ser * n_org, t_dev, per_peer), jnp.float32)

    send, dest = pl.pallas_call(
        functools.partial(pack_body, n_ser=n_ser, n_org=n_org),
        out_shape=(blocks_shape, jax.ShapeDtypeStruct((ser_dev // LANES, LANES), jnp.int32)),
        in_specs=[smem, smem, vmem, vmem],
        out_specs=(vmem, vmem),
        scratch_shapes=[pltpu.VMEM(perm.shape, jnp.int32)],
        compiler_params=params,
        name="pack",
    )(sub_size, sub_owner, residual, perm)
    recv = lax.all_to_all(send, ("ser", "org"), split_axis=0, concat_axis=0, tiled=True)
    back, log_part = pl.pallas_call(
        functools.partial(owner_body, n_ser=n_ser, n_org=n_org, ser_dev=ser_dev),
        out_shape=(blocks_shape, jax.ShapeDtypeStruct((1, share), jnp.float32)),
        in_specs=[smem, smem, vmem, vmem],
        out_specs=(vmem, vmem),
        scratch_shapes=[
            pltpu.VMEM((anchors, SLOTS), jnp.float32),
            pltpu.VMEM((SLOTS // LANES, LANES), jnp.int32),
            pltpu.VMEM((SLOTS, share), jnp.bfloat16),
            pltpu.VMEM((blocks // side, anchors, LANES), jnp.float32),
            pltpu.SMEM((3, OWNER_TILES), jnp.int32),
        ],
        compiler_params=params,
        name="owner",
    )(sub_size, sub_owner, recv, perm)
    returned = lax.all_to_all(back, ("ser", "org"), split_axis=0, concat_axis=0, tiled=True)
    whitened = pl.pallas_call(
        functools.partial(home_body, n_ser=n_ser, n_org=n_org),
        out_shape=jax.ShapeDtypeStruct((t_dev, ser_dev), jnp.float32),
        in_specs=[vmem, vmem],
        out_specs=vmem,
        compiler_params=params,
        name="home",
    )(returned, dest)
    return (whitened, log_part)


def solution(mesh):
    in_specs = (P("org", "ser"), P(), P(), P())
    out_specs = (P("org", "ser"), P("ser", "org"))
    return jax.shard_map(
        per_device, mesh=mesh, in_specs=in_specs, out_specs=out_specs, check_vma=False
    )
```

```python
import functools

import jax
import jax.numpy as jnp
from jax import lax
from jax.experimental import pallas as pl
from jax.experimental.pallas import tpu as pltpu
from jax.sharding import PartitionSpec as P

SLOTS = 2048
TILE = 256
LANES = 128
ROWS = TILE // LANES
BLOCK = 64
OWNER_TILES = SLOTS // TILE
PANEL = 16
PIVOTS = 8

epsilon = 1e-06

NN = (((1,), (0,)), ((), ()))
NT = (((1,), (1,)), ((), ()))


def dot_bf16(left, right, dims=NN):
    return lax.dot_general(left, right, dims, preferred_element_type=jnp.float32)


def dot_f32(left, right, dims=NN):
    return lax.dot_general(
        left, right, dims, precision=lax.Precision.HIGHEST, preferred_element_type=jnp.float32
    )


def as_bf16(mask):
    return jnp.where(mask, 1.0, 0.0).astype(jnp.bfloat16)


def split_three(value):
    high = value.astype(jnp.bfloat16)
    rest = value - high.astype(jnp.float32)
    middle = rest.astype(jnp.bfloat16)
    low = (rest - middle.astype(jnp.float32)).astype(jnp.bfloat16)
    return jnp.concatenate([high, middle, low], axis=0)


def join_three(value):
    rows = value.shape[0] // 3
    return value[:rows] + value[rows : 2 * rows] + value[2 * rows :]


def iota(shape, dim):
    return lax.broadcasted_iota(jnp.int32, shape, dim)


def before_in_row(width):
    return as_bf16(iota((LANES, width), 0) < iota((LANES, width), 1))


def pack_body(
    size_hbm,
    owner_hbm,
    x_hbm,
    perm_hbm,
    send_hbm,
    dest_ref,
    size_ref,
    owner_ref,
    x_ref,
    perm_ref,
    place_ref,
    send_ref,
    in_sems,
    out_sems,
    *,
    n_ser,
    n_org,
):
    loads = [
        pltpu.make_async_copy(source, target, in_sems.at[i])
        for i, (source, target) in enumerate(
            [
                (size_hbm, size_ref),
                (owner_hbm, owner_ref),
                (perm_hbm, perm_ref),
                (x_hbm, x_ref),
            ]
        )
    ]
    for load in loads:
        load.start()
    here = lax.axis_index("ser")
    n_sub = size_ref.shape[0]
    rows = perm_ref.shape[0]
    t_dev, ser_dev = x_ref.shape
    per_peer = SLOTS // n_ser
    shift = ser_dev.bit_length() - 1
    groups = ser_dev // LANES
    for load in loads[:3]:
        load.wait()

    def owner_of(row_ids):
        owner = jnp.zeros(row_ids.shape, jnp.int32)
        start = jnp.int32(0)
        for k in range(n_sub):
            owner = jnp.where(row_ids >= start, owner_ref[k], owner)
            start = start + (size_ref[k] >> 7)
        return owner

    owner_down = owner_of(iota((rows, LANES), 0))
    owner_across = owner_of(iota((1, rows), 1))
    down_wide = owner_down[:, :rows] if rows <= LANES else owner_of(iota((rows, rows), 0))
    earlier = as_bf16(
        (down_wide == owner_across) & (iota((rows, rows), 1) < iota((rows, rows), 0))
    )
    mine = as_bf16((perm_ref[...] >> shift) == here)
    in_row = dot_bf16(mine, before_in_row(LANES))
    ahead = dot_bf16(earlier, mine).astype(jnp.bfloat16)
    in_rows = dot_bf16(ahead, jnp.ones((LANES, LANES), jnp.bfloat16))
    place_ref[...] = owner_down * per_peer + (in_row + in_rows).astype(jnp.int32)

    def to_local(g, total):
        at = pl.ds(pl.multiple_of(g * 8, 8), 8)
        series = perm_ref[at, :]
        place = place_ref[at, :]
        local = series & (ser_dev - 1)
        group = jnp.where((series >> shift) == here, local >> 7, -1)
        lane = local & (LANES - 1)
        upper = (place >> 4).astype(jnp.float32)
        lower = (place & 15).astype(jnp.float32)
        lefts, rights = [], []
        for s in range(8):
            hit = iota((groups, LANES), 0) == group[s : s + 1]
            lefts.append(
                jnp.concatenate(
                    [jnp.where(hit, upper[s : s + 1], 0.0), jnp.where(hit, lower[s : s + 1], 0.0)],
                    axis=0,
                ).astype(jnp.bfloat16)
            )
            rights.append(as_bf16(iota((LANES, LANES), 0) == lane[s : s + 1]))
        return total + dot_bf16(
            jnp.concatenate(lefts, axis=1), jnp.concatenate(rights, axis=1), NT
        )

    steps = rows // 8
    found = lax.fori_loop(
        0,
        steps,
        to_local,
        jnp.zeros((2 * groups, LANES), jnp.float32),
        unroll=steps <= 8,
    )
    dest = (found[:groups] * 16.0 + found[groups:]).astype(jnp.int32)
    dest_ref[...] = dest
    loads[3].wait()
    terms = split_three(x_ref[...])

    def store(o, r):
        return pltpu.make_async_copy(
            send_ref.at[o], send_hbm.at[o * n_org + r], out_sems.at[o * n_org + r]
        )

    def pack(o, carry):
        target = iota((per_peer, LANES), 0) + o * per_peer
        pick = jnp.concatenate([as_bf16(target == dest[h : h + 1]) for h in range(groups)], axis=1)
        send_ref[o] = join_three(dot_bf16(terms, pick, NT))
        for r in range(n_org):
            store(o, r).start()
        return carry

    def finish(o, carry):
        for r in range(n_org):
            store(o, r).wait()
        return carry

    lax.fori_loop(0, n_ser, pack, 0, unroll=n_ser <= 8)
    lax.fori_loop(0, n_ser, finish, 0, unroll=n_ser <= 8)


def lane_pick(value, index):
    return jnp.take_along_axis(value, index, axis=1, mode="promise_in_bounds")


def eliminate(parts, size, whole):
    lane = iota((8, LANES), 1)
    sub = iota((8, LANES), 0)
    base = lane & (LANES - size)
    local = lane & (size - 1)
    parts = [list(part) for part in parts]
    downs = [[jnp.ones((8, LANES), jnp.float32)] * len(part) for part in parts]
    acrosses = [jnp.ones((8, LANES), jnp.float32) for _ in parts]
    tall = PANEL // 8
    count = PIVOTS
    for top in range(0, size, PANEL):
        first = top // 8
        inside = (local >= top) & (local < top + PANEL)
        panels = [part[first : first + tall] for part in parts]
        kept = [list(panel) for panel in panels]
        for j in range(top, top + PANEL, count):
            g, s = divmod(j - top, 8)
            columns = [base + (j + a) for a in range(count)]
            at = [local == j + a for a in range(count)]
            on = (local >= j) & (local < j + count)
            for p, panel in enumerate(panels):
                picked = [[lane_pick(piece, column) for column in columns] for piece in panel]
                corner = [
                    [
                        jnp.broadcast_to(picked[g][b][s + a : s + a + 1], (8, LANES))
                        for b in range(a + 1)
                    ]
                    for a in range(count)
                ]
                inv, low = [], [[None] * count for _ in range(count)]
                for k in range(count):
                    inv.append(1.0 / corner[k][k])
                    for a in range(k + 1, count):
                        low[a][k] = corner[a][k] * inv[k]
                    for a in range(k + 1, count):
                        for b in range(k + 1, a + 1):
                            corner[a][b] = corner[a][b] - low[a][k] * corner[b][k]
                rows, solved = [], [None] * count
                for a in range(count):
                    row = jnp.broadcast_to(panel[g][s + a : s + a + 1], (8, LANES))
                    row = jnp.where(on, jnp.where(at[a], 1.0, 0.0), row)
                    for b in range(a):
                        row = row - low[a][b] * rows[b]
                    rows.append(row)
                for a in reversed(range(count)):
                    row = rows[a] * inv[a]
                    for b in range(a + 1, count):
                        row = row - low[b][a] * solved[b]
                    solved[a] = row
                for v in range(tall):
                    new = jnp.where(on, 0.0, panel[v])
                    for a in range(count):
                        new = new - picked[v][a] * solved[a]
                    if v == g:
                        for a in range(count):
                            new = jnp.where(sub == s + a, solved[a], new)
                    panel[v] = new
                if not whole:
                    for v in range(g, tall):
                        ahead = (sub >= s + count) | (v > g)
                        kept[p][v] = jnp.where(ahead, panel[v], kept[p][v])
                    for a in range(count):
                        here = sub == s + a
                        pivot = corner[a][a]
                        kept[p][g] = jnp.where(here, rows[a], kept[p][g])
                        downs[p][first + g] = jnp.where(here, pivot, downs[p][first + g])
                        acrosses[p] = jnp.where(at[a], pivot, acrosses[p])
        for p, part in enumerate(parts):
            others = [i for i in range(len(part)) if i >= first + tall or (whole and i < first)]
            if others:
                zero = jnp.zeros((8, LANES), jnp.float32)
                pieces = []
                for h in range(LANES // size):
                    half = base == h * size
                    for i in range(size // 8):
                        if first <= i < first + tall:
                            pieces.append(jnp.where(half, panels[p][i - first], 0.0))
                        else:
                            pieces.append(zero)
                change = dot_f32(
                    jnp.concatenate([part[i] for i in others], axis=0),
                    jnp.concatenate(pieces, axis=0),
                )
                for n, i in enumerate(others):
                    part[i] = jnp.where(inside, 0.0, part[i]) - change[n * 8 : n * 8 + 8]
            part[first : first + tall] = panels[p] if whole else kept[p]
    return parts, downs, acrosses


def slots_body(
    size_ref,
    owner_ref,
    perm_ref,
    pick_ref,
    tile_of_ref,
    tile_ref,
    index_ref,
    *,
    n_ser,
    n_org,
    ser_dev,
):
    here = lax.axis_index("ser")
    part = lax.axis_index("org")
    n_sub = size_ref.shape[0]
    per_peer = SLOTS // n_ser
    share = SLOTS // n_org
    tiles = share // TILE
    shift = ser_dev.bit_length() - 1
    slot_rows = SLOTS // LANES
    wide = max(per_peer, LANES)

    for t in range(OWNER_TILES):
        tile_ref[0, t] = jnp.int32(-1)
        tile_ref[1, t] = jnp.int32(0)
        tile_ref[2, t] = jnp.int32(0)
    at = jnp.int32(0)
    first = jnp.int32(0)
    for k in range(n_sub):
        count = size_ref[k] >> 8
        held = jnp.where(owner_ref[k] == here, count, 0)

        def put(i, carry, at=at, first=first, held=held):
            tile_ref[0, at + i] = first + i
            tile_ref[1, at + i] = at
            tile_ref[2, at + i] = at + held
            return carry

        lax.fori_loop(0, held, put, 0)
        at = at + held
        first = first + count

    pieces = []
    for t in range(OWNER_TILES):
        place = tile_ref[0, t]
        rows = perm_ref[pl.ds(jnp.maximum(place, 0) * ROWS, ROWS), :]
        pieces.append(jnp.where(place >= 0, rows, -1))
    source = jnp.concatenate(pieces, axis=0) >> shift
    from_peer = jnp.concatenate([as_bf16(source == d) for d in range(n_ser)], axis=0)
    in_row = dot_bf16(from_peer, before_in_row(LANES))
    row_total = dot_bf16(from_peer, jnp.ones((LANES, wide), jnp.bfloat16)).astype(jnp.bfloat16)
    span = n_ser * slot_rows
    left, right = iota((span, span), 0), iota((span, span), 1)
    ahead = as_bf16((left // slot_rows == right // slot_rows) & (right < left))
    base = dot_bf16(ahead, row_total)[:, :LANES]
    rank = jnp.zeros((slot_rows, LANES), jnp.float32)
    for d in range(n_ser):
        rows = slice(d * slot_rows, (d + 1) * slot_rows)
        rank = jnp.where(source == d, in_row[rows] + base[rows], rank)
    index_ref[...] = jnp.where(source >= 0, source * per_peer + rank.astype(jnp.int32), -1)
    left, right = iota((OWNER_TILES * n_ser, span), 0), iota((OWNER_TILES * n_ser, span), 1)
    through = as_bf16(
        (left % n_ser == right // slot_rows)
        & (right % slot_rows < ROWS * (left // n_ser) + ROWS)
    )
    ends = dot_bf16(through, row_total).astype(jnp.int32)[:, :per_peer]
    tile_of = jnp.zeros((n_ser, per_peer), jnp.int32)
    for t in range(OWNER_TILES):
        tile_of += (iota((n_ser, per_peer), 1) >= ends[t * n_ser : (t + 1) * n_ser]).astype(
            jnp.int32
        )
    tile_of = jnp.concatenate([tile_of[d : d + 1] for d in range(n_ser)], axis=1)
    tile_of_ref[...] = tile_of

    for i in range(share // LANES):
        row = index_ref[pl.ds(part * (tiles * ROWS) + i, 1), :]
        pick_ref[:, i * LANES : (i + 1) * LANES] = as_bf16(iota((SLOTS, LANES), 0) == row)


def owner_body(
    recv_ref,
    pick_ref,
    tile_of_ref,
    tile_ref,
    back_ref,
    log_ref,
    all_ref,
    inverse_ref,
    *,
    n_ser,
    n_org,
):
    part = lax.axis_index("org")
    t_dev = recv_ref.shape[1]
    anchors = t_dev * n_org
    per_peer = SLOTS // n_ser
    share = SLOTS // n_org
    tiles = share // TILE

    for d in range(n_ser):
        for r in range(n_org):
            all_ref[r * t_dev : (r + 1) * t_dev, d * per_peer : (d + 1) * per_peer] = recv_ref[
                d * n_org + r
            ]

    tile_of = tile_of_ref[...]

    block = all_ref[...]
    spread = jnp.sum(block * block, axis=0, keepdims=True) * (1.0 / anchors)
    scaled = block * jnp.where(spread > 0, lax.rsqrt(spread), 0.0)
    own = spread / (spread + epsilon)
    fourth = jnp.sum(jnp.square(scaled * scaled), axis=0, keepdims=True) * (1.0 / anchors)
    in_tree, ahead_of, filled = [], [], []
    for u in range(tiles):
        t = part * tiles + u
        low, high = tile_ref[1, t], tile_ref[2, t]
        filled.append(tile_ref[0, t] >= 0)
        in_tree.append((tile_of >= low) & (tile_of < high))
        ahead_of.append((tile_of >= low) & (tile_of < t))
    terms = split_three(scaled)
    weighted = split_three(scaled * own)
    products = dot_bf16(
        jnp.concatenate(
            [weighted * as_bf16(mask) for mask in in_tree]
            + [terms * as_bf16(mask) for mask in ahead_of],
            axis=0,
        ),
        terms,
        NT,
    )
    grams = []
    for u in range(2 * tiles):
        piece = join_three(products[u * 3 * anchors : (u + 1) * 3 * anchors])
        grams.append(
            piece[:, 2 * anchors :] + piece[:, anchors : 2 * anchors] + piece[:, :anchors]
        )
    unit = iota((anchors, anchors), 0) == iota((anchors, anchors), 1)
    shrink = []
    for u in range(tiles):
        dual = grams[u] * (1.0 / anchors)
        own_square = jnp.where(in_tree[u], own * own, 0.0)
        square = dual * dual
        total = lambda value: jnp.sum(
            jnp.sum(value, axis=0, keepdims=True), axis=1, keepdims=True
        )
        lower = total(square) - total(own_square)
        upper = total(jnp.where(unit, square, 0.0)) * anchors - total(own_square * fourth)
        upper = (upper - lower) / (anchors - 1)
        shrink.append(jnp.where(filled[u], jnp.minimum(upper / jnp.where(filled[u], lower, 1.0), 1.0), 1.0))

    levels = split_three(jnp.broadcast_to(spread, (16, SLOTS)))
    found = dot_bf16(jnp.concatenate([terms, levels], axis=0), pick_ref[...])
    mine = join_three(found[: 3 * anchors])
    my_spread = join_three(found[3 * anchors :])[:1]
    mine_down = mine.T

    per_tile = TILE // BLOCK
    blocks = share // BLOCK
    side = LANES // anchors
    rows_of = lambda b: slice(b * BLOCK, (b + 1) * BLOCK)
    for u in range(tiles):
        prior = grams[tiles + u]
        gain = (1.0 - shrink[u]) * (1.0 / anchors)
        for v in range(per_tile):
            b = u * per_tile + v
            inverse_ref[b // side, :, (b % side) * anchors : (b % side + 1) * anchors] = (
                jnp.where(unit, shrink[u], 0.0) + gain * prior
            )
            if v < per_tile - 1:
                piece = mine[:, rows_of(b)]
                prior = prior + dot_f32(piece, piece, NT)

    inverses, _, _ = eliminate(
        [
            [inverse_ref[p, i * 8 : (i + 1) * 8, :] for i in range(anchors // 8)]
            for p in range(blocks // side)
        ],
        anchors,
        whole=True,
    )
    inverses = [jnp.concatenate(rows, axis=0) for rows in inverses]

    diagonal = iota((BLOCK, BLOCK), 0) == iota((BLOCK, BLOCK), 1)
    solved, weights = [], []
    for b in range(blocks):
        gain = (1.0 - shrink[b // per_tile]) * (1.0 / anchors)
        inverse = inverses[b // side][:, (b % side) * anchors : (b % side + 1) * anchors]
        solved.append(dot_f32(inverse, mine[:, rows_of(b)]))
        weights.append(
            jnp.where(diagonal, 1.0, 0.0) + gain * dot_f32(mine_down[rows_of(b)], solved[b])
        )
    pairs = [jnp.concatenate(weights[b : b + 2], axis=1) for b in range(0, blocks, 2)]
    lowers, downs, acrosses = eliminate(
        [[pair[i * 8 : (i + 1) * 8] for i in range(BLOCK // 8)] for pair in pairs],
        BLOCK,
        whole=False,
    )
    keep = iota((BLOCK, LANES), 0) >= (iota((BLOCK, LANES), 1) & (BLOCK - 1))
    done, logs = [], []
    for p in range(blocks // 2):
        lower = jnp.concatenate(
            [row * lax.rsqrt(pivot) for row, pivot in zip(lowers[p], downs[p])], axis=0
        )
        lower = jnp.where(keep, lower, 0.0)
        for h in range(2):
            b = 2 * p + h
            u = b // per_tile
            half = slice(h * BLOCK, (h + 1) * BLOCK)
            done.append(dot_f32(solved[b], lower[:, half], NT) * jnp.sqrt(shrink[u]))
            level = acrosses[p][:1, half] * my_spread[:, rows_of(b)] * shrink[u]
            logs.append(jnp.where(filled[u], 0.5 * jnp.log(level), 0.0))
    log_ref[...] = jnp.concatenate(logs, axis=1)
    terms = split_three(jnp.concatenate(done, axis=1))

    for d in range(n_ser):
        columns = join_three(
            dot_bf16(terms, pick_ref[d * per_peer : (d + 1) * per_peer, :], NT)
        )
        for r in range(n_org):
            back_ref[d * n_org + r] = columns[r * t_dev : (r + 1) * t_dev]


def home_body(back_ref, dest_ref, out_ref, *, n_ser, n_org):
    per_peer = back_ref.shape[2]
    pieces = []
    for o in range(n_ser):
        piece = back_ref[o * n_org]
        for q in range(1, n_org):
            piece = piece + back_ref[o * n_org + q]
        pieces.append(piece)
    terms = split_three(jnp.concatenate(pieces, axis=1))
    groups = dest_ref.shape[0]
    step = 2
    for h in range(0, groups, step):
        pick = jnp.concatenate(
            [
                as_bf16(iota((SLOTS, LANES), 0) == dest_ref[h + i : h + i + 1, :])
                for i in range(step)
            ],
            axis=1,
        )
        out_ref[:, h * LANES : (h + step) * LANES] = join_three(dot_bf16(terms, pick))


def per_device(residual, sub_size, sub_owner, series_perm):
    n_ser = lax.axis_size("ser")
    n_org = lax.axis_size("org")
    t_dev, ser_dev = residual.shape
    anchors = t_dev * n_org
    per_peer = SLOTS // n_ser
    share = SLOTS // n_org
    blocks = share // BLOCK
    side = LANES // anchors
    perm = series_perm.reshape(-1, LANES)
    to_hbm = lambda value: pltpu.with_memory_space_constraint(value, pltpu.HBM)
    vmem = pl.BlockSpec(memory_space=pltpu.VMEM)
    smem = pl.BlockSpec(memory_space=pltpu.SMEM)
    hbm = pl.BlockSpec(memory_space=pltpu.HBM)
    params = pltpu.CompilerParams(vmem_limit_bytes=48 * 1024 * 1024)
    blocks_shape = jax.ShapeDtypeStruct((n_ser * n_org, t_dev, per_peer), jnp.float32)

    send, dest = pl.pallas_call(
        functools.partial(pack_body, n_ser=n_ser, n_org=n_org),
        out_shape=(blocks_shape, jax.ShapeDtypeStruct((ser_dev // LANES, LANES), jnp.int32)),
        in_specs=[hbm, hbm, hbm, hbm],
        out_specs=(hbm, vmem),
        scratch_shapes=[
            pltpu.SMEM(sub_size.shape, jnp.int32),
            pltpu.SMEM(sub_owner.shape, jnp.int32),
            pltpu.VMEM(residual.shape, jnp.float32),
            pltpu.VMEM(perm.shape, jnp.int32),
            pltpu.VMEM(perm.shape, jnp.int32),
            pltpu.VMEM((n_ser, t_dev, per_peer), jnp.float32),
            pltpu.SemaphoreType.DMA((4,)),
            pltpu.SemaphoreType.DMA((n_ser * n_org,)),
        ],
        compiler_params=params,
        name="pack",
    )(to_hbm(sub_size), to_hbm(sub_owner), to_hbm(residual), to_hbm(perm))
    recv = lax.all_to_all(send, ("ser", "org"), split_axis=0, concat_axis=0, tiled=True)
    pick, tile_of, tile = pl.pallas_call(
        functools.partial(slots_body, n_ser=n_ser, n_org=n_org, ser_dev=ser_dev),
        out_shape=(
            jax.ShapeDtypeStruct((SLOTS, share), jnp.bfloat16),
            jax.ShapeDtypeStruct((1, SLOTS), jnp.int32),
            jax.ShapeDtypeStruct((3, OWNER_TILES), jnp.int32),
        ),
        in_specs=[smem, smem, vmem],
        out_specs=(vmem, vmem, smem),
        scratch_shapes=[pltpu.VMEM((SLOTS // LANES, LANES), jnp.int32)],
        compiler_params=params,
        cost_estimate=pl.CostEstimate(
            flops=4_000_000_000, bytes_accessed=4_000_000, transcendentals=0
        ),
        name="slots",
    )(sub_size, sub_owner, perm)
    back, log_part = pl.pallas_call(
        functools.partial(owner_body, n_ser=n_ser, n_org=n_org),
        out_shape=(blocks_shape, jax.ShapeDtypeStruct((1, share), jnp.float32)),
        in_specs=[vmem, vmem, vmem, smem],
        out_specs=(vmem, vmem),
        scratch_shapes=[
            pltpu.VMEM((anchors, SLOTS), jnp.float32),
            pltpu.VMEM((blocks // side, anchors, LANES), jnp.float32),
        ],
        compiler_params=params,
        name="owner",
    )(recv, pick, tile_of, tile)
    returned = lax.all_to_all(back, ("ser", "org"), split_axis=0, concat_axis=0, tiled=True)
    whitened = pl.pallas_call(
        functools.partial(home_body, n_ser=n_ser, n_org=n_org),
        out_shape=jax.ShapeDtypeStruct((t_dev, ser_dev), jnp.float32),
        in_specs=[vmem, vmem],
        out_specs=vmem,
        compiler_params=params,
        name="home",
    )(returned, dest)
    return (whitened, log_part)


def solution(mesh):
    in_specs = (P("org", "ser"), P(), P(), P())
    out_specs = (P("org", "ser"), P("ser", "org"))
    return jax.shard_map(
        per_device, mesh=mesh, in_specs=in_specs, out_specs=out_specs, check_vma=False
    )
```

```python
import functools

import jax
import jax.numpy as jnp
from jax import lax
from jax.experimental import pallas as pl
from jax.experimental.pallas import tpu as pltpu
from jax.sharding import PartitionSpec as P

SLOTS = 2048
TILE = 256
LANES = 128
ROWS = TILE // LANES
BLOCK = 64
OWNER_TILES = SLOTS // TILE
PANEL = 16
PIVOTS = 8

epsilon = 1e-06

NN = (((1,), (0,)), ((), ()))
NT = (((1,), (1,)), ((), ()))


def dot_bf16(left, right, dims=NN):
    return lax.dot_general(left, right, dims, preferred_element_type=jnp.float32)


def dot_f32(left, right, dims=NN):
    return lax.dot_general(
        left, right, dims, precision=lax.Precision.HIGHEST, preferred_element_type=jnp.float32
    )


def as_bf16(mask):
    return jnp.where(mask, 1.0, 0.0).astype(jnp.bfloat16)


def split_three(value):
    high = value.astype(jnp.bfloat16)
    rest = value - high.astype(jnp.float32)
    middle = rest.astype(jnp.bfloat16)
    low = (rest - middle.astype(jnp.float32)).astype(jnp.bfloat16)
    return jnp.concatenate([high, middle, low], axis=0)


def join_three(value):
    rows = value.shape[0] // 3
    return value[:rows] + value[rows : 2 * rows] + value[2 * rows :]


def iota(shape, dim):
    return lax.broadcasted_iota(jnp.int32, shape, dim)


def before_in_row(width):
    return as_bf16(iota((LANES, width), 0) < iota((LANES, width), 1))


def pack_body(
    size_hbm,
    owner_hbm,
    x_hbm,
    perm_hbm,
    send_hbm,
    dest_ref,
    size_ref,
    owner_ref,
    x_ref,
    perm_ref,
    place_ref,
    send_ref,
    in_sems,
    out_sems,
    *,
    n_ser,
    n_org,
):
    loads = [
        pltpu.make_async_copy(source, target, in_sems.at[i])
        for i, (source, target) in enumerate(
            [
                (size_hbm, size_ref),
                (owner_hbm, owner_ref),
                (perm_hbm, perm_ref),
                (x_hbm, x_ref),
            ]
        )
    ]
    for load in loads:
        load.start()
    here = lax.axis_index("ser")
    n_sub = size_ref.shape[0]
    rows = perm_ref.shape[0]
    t_dev, ser_dev = x_ref.shape
    per_peer = SLOTS // n_ser
    shift = ser_dev.bit_length() - 1
    groups = ser_dev // LANES
    for load in loads[:3]:
        load.wait()

    def owner_of(row_ids):
        owner = jnp.zeros(row_ids.shape, jnp.int32)
        start = jnp.int32(0)
        for k in range(n_sub):
            owner = jnp.where(row_ids >= start, owner_ref[k], owner)
            start = start + (size_ref[k] >> 7)
        return owner

    owner_down = owner_of(iota((rows, LANES), 0))
    owner_across = owner_of(iota((1, rows), 1))
    down_wide = owner_down[:, :rows] if rows <= LANES else owner_of(iota((rows, rows), 0))
    earlier = as_bf16(
        (down_wide == owner_across) & (iota((rows, rows), 1) < iota((rows, rows), 0))
    )
    mine = as_bf16((perm_ref[...] >> shift) == here)
    in_row = dot_bf16(mine, before_in_row(LANES))
    ahead = dot_bf16(earlier, mine).astype(jnp.bfloat16)
    in_rows = dot_bf16(ahead, jnp.ones((LANES, LANES), jnp.bfloat16))
    place_ref[...] = owner_down * per_peer + (in_row + in_rows).astype(jnp.int32)

    def to_local(g, total):
        at = pl.ds(pl.multiple_of(g * 8, 8), 8)
        series = perm_ref[at, :]
        place = place_ref[at, :]
        local = series & (ser_dev - 1)
        group = jnp.where((series >> shift) == here, local >> 7, -1)
        lane = local & (LANES - 1)
        upper = (place >> 4).astype(jnp.float32)
        lower = (place & 15).astype(jnp.float32)
        lefts, rights = [], []
        for s in range(8):
            hit = iota((groups, LANES), 0) == group[s : s + 1]
            lefts.append(
                jnp.concatenate(
                    [jnp.where(hit, upper[s : s + 1], 0.0), jnp.where(hit, lower[s : s + 1], 0.0)],
                    axis=0,
                ).astype(jnp.bfloat16)
            )
            rights.append(as_bf16(iota((LANES, LANES), 0) == lane[s : s + 1]))
        return total + dot_bf16(
            jnp.concatenate(lefts, axis=1), jnp.concatenate(rights, axis=1), NT
        )

    steps = rows // 8
    found = lax.fori_loop(
        0,
        steps,
        to_local,
        jnp.zeros((2 * groups, LANES), jnp.float32),
        unroll=steps <= 8,
    )
    dest = (found[:groups] * 16.0 + found[groups:]).astype(jnp.int32)
    dest_ref[...] = dest
    loads[3].wait()
    terms = split_three(x_ref[...])

    def store(o, r):
        return pltpu.make_async_copy(
            send_ref.at[o], send_hbm.at[o], out_sems.at[o]
        )

    def pack(o, carry):
        target = iota((per_peer, LANES), 0) + o * per_peer
        pick = jnp.concatenate([as_bf16(target == dest[h : h + 1]) for h in range(groups)], axis=1)
        send_ref[o] = join_three(dot_bf16(terms, pick, NT))
        store(o, 0).start()
        return carry

    def finish(o, carry):
        store(o, 0).wait()
        return carry

    lax.fori_loop(0, n_ser, pack, 0, unroll=n_ser <= 8)
    lax.fori_loop(0, n_ser, finish, 0, unroll=n_ser <= 8)


def lane_pick(value, index):
    return jnp.take_along_axis(value, index, axis=1, mode="promise_in_bounds")


def eliminate(parts, size, whole):
    lane = iota((8, LANES), 1)
    sub = iota((8, LANES), 0)
    base = lane & (LANES - size)
    local = lane & (size - 1)
    parts = [list(part) for part in parts]
    downs = [[jnp.ones((8, LANES), jnp.float32)] * len(part) for part in parts]
    acrosses = [jnp.ones((8, LANES), jnp.float32) for _ in parts]
    tall = PANEL // 8
    count = PIVOTS
    for top in range(0, size, PANEL):
        first = top // 8
        inside = (local >= top) & (local < top + PANEL)
        panels = [part[first : first + tall] for part in parts]
        kept = [list(panel) for panel in panels]
        for j in range(top, top + PANEL, count):
            g, s = divmod(j - top, 8)
            columns = [base + (j + a) for a in range(count)]
            at = [local == j + a for a in range(count)]
            on = (local >= j) & (local < j + count)
            for p, panel in enumerate(panels):
                picked = [[lane_pick(piece, column) for column in columns] for piece in panel]
                corner = [
                    [
                        jnp.broadcast_to(picked[g][b][s + a : s + a + 1], (8, LANES))
                        for b in range(a + 1)
                    ]
                    for a in range(count)
                ]
                inv, low = [], [[None] * count for _ in range(count)]
                for k in range(count):
                    inv.append(1.0 / corner[k][k])
                    for a in range(k + 1, count):
                        low[a][k] = corner[a][k] * inv[k]
                    for a in range(k + 1, count):
                        for b in range(k + 1, a + 1):
                            corner[a][b] = corner[a][b] - low[a][k] * corner[b][k]
                rows, solved = [], [None] * count
                for a in range(count):
                    row = jnp.broadcast_to(panel[g][s + a : s + a + 1], (8, LANES))
                    row = jnp.where(on, jnp.where(at[a], 1.0, 0.0), row)
                    for b in range(a):
                        row = row - low[a][b] * rows[b]
                    rows.append(row)
                for a in reversed(range(count)):
                    row = rows[a] * inv[a]
                    for b in range(a + 1, count):
                        row = row - low[b][a] * solved[b]
                    solved[a] = row
                for v in range(tall):
                    new = jnp.where(on, 0.0, panel[v])
                    for a in range(count):
                        new = new - picked[v][a] * solved[a]
                    if v == g:
                        for a in range(count):
                            new = jnp.where(sub == s + a, solved[a], new)
                    panel[v] = new
                if not whole:
                    for v in range(g, tall):
                        ahead = (sub >= s + count) | (v > g)
                        kept[p][v] = jnp.where(ahead, panel[v], kept[p][v])
                    for a in range(count):
                        here = sub == s + a
                        pivot = corner[a][a]
                        kept[p][g] = jnp.where(here, rows[a], kept[p][g])
                        downs[p][first + g] = jnp.where(here, pivot, downs[p][first + g])
                        acrosses[p] = jnp.where(at[a], pivot, acrosses[p])
        for p, part in enumerate(parts):
            others = [i for i in range(len(part)) if i >= first + tall or (whole and i < first)]
            if others:
                zero = jnp.zeros((8, LANES), jnp.float32)
                pieces = []
                for h in range(LANES // size):
                    half = base == h * size
                    for i in range(size // 8):
                        if first <= i < first + tall:
                            pieces.append(jnp.where(half, panels[p][i - first], 0.0))
                        else:
                            pieces.append(zero)
                change = dot_f32(
                    jnp.concatenate([part[i] for i in others], axis=0),
                    jnp.concatenate(pieces, axis=0),
                )
                for n, i in enumerate(others):
                    part[i] = jnp.where(inside, 0.0, part[i]) - change[n * 8 : n * 8 + 8]
            part[first : first + tall] = panels[p] if whole else kept[p]
    return parts, downs, acrosses


def slots_body(
    size_ref,
    owner_ref,
    perm_ref,
    pick_ref,
    tile_of_ref,
    tile_ref,
    index_ref,
    *,
    n_ser,
    n_org,
    ser_dev,
):
    here = lax.axis_index("ser")
    part = lax.axis_index("org")
    n_sub = size_ref.shape[0]
    per_peer = SLOTS // n_ser
    share = SLOTS // n_org
    tiles = share // TILE
    shift = ser_dev.bit_length() - 1
    slot_rows = SLOTS // LANES
    wide = max(per_peer, LANES)

    for t in range(OWNER_TILES):
        tile_ref[0, t] = jnp.int32(-1)
        tile_ref[1, t] = jnp.int32(0)
        tile_ref[2, t] = jnp.int32(0)
    at = jnp.int32(0)
    first = jnp.int32(0)
    for k in range(n_sub):
        count = size_ref[k] >> 8
        held = jnp.where(owner_ref[k] == here, count, 0)

        def put(i, carry, at=at, first=first, held=held):
            tile_ref[0, at + i] = first + i
            tile_ref[1, at + i] = at
            tile_ref[2, at + i] = at + held
            return carry

        lax.fori_loop(0, held, put, 0)
        at = at + held
        first = first + count

    pieces = []
    for t in range(OWNER_TILES):
        place = tile_ref[0, t]
        rows = perm_ref[pl.ds(jnp.maximum(place, 0) * ROWS, ROWS), :]
        pieces.append(jnp.where(place >= 0, rows, -1))
    source = jnp.concatenate(pieces, axis=0) >> shift
    from_peer = jnp.concatenate([as_bf16(source == d) for d in range(n_ser)], axis=0)
    in_row = dot_bf16(from_peer, before_in_row(LANES))
    row_total = dot_bf16(from_peer, jnp.ones((LANES, wide), jnp.bfloat16)).astype(jnp.bfloat16)
    span = n_ser * slot_rows
    left, right = iota((span, span), 0), iota((span, span), 1)
    ahead = as_bf16((left // slot_rows == right // slot_rows) & (right < left))
    base = dot_bf16(ahead, row_total)[:, :LANES]
    rank = jnp.zeros((slot_rows, LANES), jnp.float32)
    for d in range(n_ser):
        rows = slice(d * slot_rows, (d + 1) * slot_rows)
        rank = jnp.where(source == d, in_row[rows] + base[rows], rank)
    index_ref[...] = jnp.where(source >= 0, source * per_peer + rank.astype(jnp.int32), -1)
    left, right = iota((OWNER_TILES * n_ser, span), 0), iota((OWNER_TILES * n_ser, span), 1)
    through = as_bf16(
        (left % n_ser == right // slot_rows)
        & (right % slot_rows < ROWS * (left // n_ser) + ROWS)
    )
    ends = dot_bf16(through, row_total).astype(jnp.int32)[:, :per_peer]
    tile_of = jnp.zeros((n_ser, per_peer), jnp.int32)
    for t in range(OWNER_TILES):
        tile_of += (iota((n_ser, per_peer), 1) >= ends[t * n_ser : (t + 1) * n_ser]).astype(
            jnp.int32
        )
    tile_of = jnp.concatenate([tile_of[d : d + 1] for d in range(n_ser)], axis=1)
    tile_of_ref[...] = tile_of

    for i in range(share // LANES):
        row = index_ref[pl.ds(part * (tiles * ROWS) + i, 1), :]
        pick_ref[:, i * LANES : (i + 1) * LANES] = as_bf16(iota((SLOTS, LANES), 0) == row)


def owner_body(
    recv_ref,
    pick_ref,
    tile_of_ref,
    tile_ref,
    back_ref,
    log_ref,
    all_ref,
    inverse_ref,
    *,
    n_ser,
    n_org,
):
    part = lax.axis_index("org")
    t_dev = recv_ref.shape[1]
    anchors = t_dev * n_org
    per_peer = SLOTS // n_ser
    share = SLOTS // n_org
    tiles = share // TILE

    for d in range(n_ser):
        for r in range(n_org):
            all_ref[r * t_dev : (r + 1) * t_dev, d * per_peer : (d + 1) * per_peer] = recv_ref[
                r * n_ser + d
            ]

    tile_of = tile_of_ref[...]

    block = all_ref[...]
    spread = jnp.sum(block * block, axis=0, keepdims=True) * (1.0 / anchors)
    scaled = block * jnp.where(spread > 0, lax.rsqrt(spread), 0.0)
    own = spread / (spread + epsilon)
    fourth = jnp.sum(jnp.square(scaled * scaled), axis=0, keepdims=True) * (1.0 / anchors)
    in_tree, ahead_of, filled = [], [], []
    for u in range(tiles):
        t = part * tiles + u
        low, high = tile_ref[1, t], tile_ref[2, t]
        filled.append(tile_ref[0, t] >= 0)
        in_tree.append((tile_of >= low) & (tile_of < high))
        ahead_of.append((tile_of >= low) & (tile_of < t))
    terms = split_three(scaled)
    weighted = split_three(scaled * own)
    products = dot_bf16(
        jnp.concatenate(
            [weighted * as_bf16(mask) for mask in in_tree]
            + [terms * as_bf16(mask) for mask in ahead_of],
            axis=0,
        ),
        terms,
        NT,
    )
    grams = []
    for u in range(2 * tiles):
        piece = join_three(products[u * 3 * anchors : (u + 1) * 3 * anchors])
        grams.append(
            piece[:, 2 * anchors :] + piece[:, anchors : 2 * anchors] + piece[:, :anchors]
        )
    unit = iota((anchors, anchors), 0) == iota((anchors, anchors), 1)
    shrink = []
    for u in range(tiles):
        dual = grams[u] * (1.0 / anchors)
        own_square = jnp.where(in_tree[u], own * own, 0.0)
        square = dual * dual
        total = lambda value: jnp.sum(
            jnp.sum(value, axis=0, keepdims=True), axis=1, keepdims=True
        )
        lower = total(square) - total(own_square)
        upper = total(jnp.where(unit, square, 0.0)) * anchors - total(own_square * fourth)
        upper = (upper - lower) / (anchors - 1)
        shrink.append(jnp.where(filled[u], jnp.minimum(upper / jnp.where(filled[u], lower, 1.0), 1.0), 1.0))

    levels = split_three(jnp.broadcast_to(spread, (16, SLOTS)))
    found = dot_bf16(jnp.concatenate([terms, levels], axis=0), pick_ref[...])
    mine = join_three(found[: 3 * anchors])
    my_spread = join_three(found[3 * anchors :])[:1]
    mine_down = mine.T

    per_tile = TILE // BLOCK
    blocks = share // BLOCK
    side = LANES // anchors
    rows_of = lambda b: slice(b * BLOCK, (b + 1) * BLOCK)
    for u in range(tiles):
        prior = grams[tiles + u]
        gain = (1.0 - shrink[u]) * (1.0 / anchors)
        for v in range(per_tile):
            b = u * per_tile + v
            inverse_ref[b // side, :, (b % side) * anchors : (b % side + 1) * anchors] = (
                jnp.where(unit, shrink[u], 0.0) + gain * prior
            )
            if v < per_tile - 1:
                piece = mine[:, rows_of(b)]
                prior = prior + dot_f32(piece, piece, NT)

    inverses, _, _ = eliminate(
        [
            [inverse_ref[p, i * 8 : (i + 1) * 8, :] for i in range(anchors // 8)]
            for p in range(blocks // side)
        ],
        anchors,
        whole=True,
    )
    inverses = [jnp.concatenate(rows, axis=0) for rows in inverses]

    diagonal = iota((BLOCK, BLOCK), 0) == iota((BLOCK, BLOCK), 1)
    solved, weights = [], []
    for b in range(blocks):
        gain = (1.0 - shrink[b // per_tile]) * (1.0 / anchors)
        inverse = inverses[b // side][:, (b % side) * anchors : (b % side + 1) * anchors]
        solved.append(dot_f32(inverse, mine[:, rows_of(b)]))
        weights.append(
            jnp.where(diagonal, 1.0, 0.0) + gain * dot_f32(mine_down[rows_of(b)], solved[b])
        )
    pairs = [jnp.concatenate(weights[b : b + 2], axis=1) for b in range(0, blocks, 2)]
    lowers, downs, acrosses = eliminate(
        [[pair[i * 8 : (i + 1) * 8] for i in range(BLOCK // 8)] for pair in pairs],
        BLOCK,
        whole=False,
    )
    keep = iota((BLOCK, LANES), 0) >= (iota((BLOCK, LANES), 1) & (BLOCK - 1))
    done, logs = [], []
    for p in range(blocks // 2):
        lower = jnp.concatenate(
            [row * lax.rsqrt(pivot) for row, pivot in zip(lowers[p], downs[p])], axis=0
        )
        lower = jnp.where(keep, lower, 0.0)
        for h in range(2):
            b = 2 * p + h
            u = b // per_tile
            half = slice(h * BLOCK, (h + 1) * BLOCK)
            done.append(dot_f32(solved[b], lower[:, half], NT) * jnp.sqrt(shrink[u]))
            level = acrosses[p][:1, half] * my_spread[:, rows_of(b)] * shrink[u]
            logs.append(jnp.where(filled[u], 0.5 * jnp.log(level), 0.0))
    log_ref[...] = jnp.concatenate(logs, axis=1)
    terms = split_three(jnp.concatenate(done, axis=1))

    for d in range(n_ser):
        columns = join_three(
            dot_bf16(terms, pick_ref[d * per_peer : (d + 1) * per_peer, :], NT)
        )
        for r in range(n_org):
            back_ref[d * n_org + r] = columns[r * t_dev : (r + 1) * t_dev]


def home_body(back_ref, dest_ref, out_ref, *, n_ser, n_org):
    per_peer = back_ref.shape[2]
    pieces = []
    for o in range(n_ser):
        piece = back_ref[o * n_org]
        for q in range(1, n_org):
            piece = piece + back_ref[o * n_org + q]
        pieces.append(piece)
    terms = split_three(jnp.concatenate(pieces, axis=1))
    groups = dest_ref.shape[0]
    step = 2
    for h in range(0, groups, step):
        pick = jnp.concatenate(
            [
                as_bf16(iota((SLOTS, LANES), 0) == dest_ref[h + i : h + i + 1, :])
                for i in range(step)
            ],
            axis=1,
        )
        out_ref[:, h * LANES : (h + step) * LANES] = join_three(dot_bf16(terms, pick))


def per_device(residual, sub_size, sub_owner, series_perm):
    n_ser = lax.axis_size("ser")
    n_org = lax.axis_size("org")
    t_dev, ser_dev = residual.shape
    anchors = t_dev * n_org
    per_peer = SLOTS // n_ser
    share = SLOTS // n_org
    blocks = share // BLOCK
    side = LANES // anchors
    perm = series_perm.reshape(-1, LANES)
    to_hbm = lambda value: pltpu.with_memory_space_constraint(value, pltpu.HBM)
    vmem = pl.BlockSpec(memory_space=pltpu.VMEM)
    smem = pl.BlockSpec(memory_space=pltpu.SMEM)
    hbm = pl.BlockSpec(memory_space=pltpu.HBM)
    params = pltpu.CompilerParams(vmem_limit_bytes=48 * 1024 * 1024)
    blocks_shape = jax.ShapeDtypeStruct((n_ser * n_org, t_dev, per_peer), jnp.float32)

    send, dest = pl.pallas_call(
        functools.partial(pack_body, n_ser=n_ser, n_org=n_org),
        out_shape=(jax.ShapeDtypeStruct((n_ser, t_dev, per_peer), jnp.float32), jax.ShapeDtypeStruct((ser_dev // LANES, LANES), jnp.int32)),
        in_specs=[hbm, hbm, hbm, hbm],
        out_specs=(hbm, vmem),
        scratch_shapes=[
            pltpu.SMEM(sub_size.shape, jnp.int32),
            pltpu.SMEM(sub_owner.shape, jnp.int32),
            pltpu.VMEM(residual.shape, jnp.float32),
            pltpu.VMEM(perm.shape, jnp.int32),
            pltpu.VMEM(perm.shape, jnp.int32),
            pltpu.VMEM((n_ser, t_dev, per_peer), jnp.float32),
            pltpu.SemaphoreType.DMA((4,)),
            pltpu.SemaphoreType.DMA((n_ser * n_org,)),
        ],
        compiler_params=params,
        name="pack",
    )(to_hbm(sub_size), to_hbm(sub_owner), to_hbm(residual), to_hbm(perm))
    recv = lax.all_to_all(send, "ser", split_axis=0, concat_axis=0, tiled=True)
    recv = lax.all_gather(recv, "org", axis=0, tiled=True)
    pick, tile_of, tile = pl.pallas_call(
        functools.partial(slots_body, n_ser=n_ser, n_org=n_org, ser_dev=ser_dev),
        out_shape=(
            jax.ShapeDtypeStruct((SLOTS, share), jnp.bfloat16),
            jax.ShapeDtypeStruct((1, SLOTS), jnp.int32),
            jax.ShapeDtypeStruct((3, OWNER_TILES), jnp.int32),
        ),
        in_specs=[smem, smem, vmem],
        out_specs=(vmem, vmem, smem),
        scratch_shapes=[pltpu.VMEM((SLOTS // LANES, LANES), jnp.int32)],
        compiler_params=params,
        cost_estimate=pl.CostEstimate(
            flops=4_000_000_000, bytes_accessed=4_000_000, transcendentals=0
        ),
        name="slots",
    )(sub_size, sub_owner, perm)
    back, log_part = pl.pallas_call(
        functools.partial(owner_body, n_ser=n_ser, n_org=n_org),
        out_shape=(blocks_shape, jax.ShapeDtypeStruct((1, share), jnp.float32)),
        in_specs=[vmem, vmem, vmem, smem],
        out_specs=(vmem, vmem),
        scratch_shapes=[
            pltpu.VMEM((anchors, SLOTS), jnp.float32),
            pltpu.VMEM((blocks // side, anchors, LANES), jnp.float32),
        ],
        compiler_params=params,
        name="owner",
    )(recv, pick, tile_of, tile)
    returned = lax.all_to_all(back, ("ser", "org"), split_axis=0, concat_axis=0, tiled=True)
    whitened = pl.pallas_call(
        functools.partial(home_body, n_ser=n_ser, n_org=n_org),
        out_shape=jax.ShapeDtypeStruct((t_dev, ser_dev), jnp.float32),
        in_specs=[vmem, vmem],
        out_specs=vmem,
        compiler_params=params,
        name="home",
    )(returned, dest)
    return (whitened, log_part)


def solution(mesh):
    in_specs = (P("org", "ser"), P(), P(), P())
    out_specs = (P("org", "ser"), P("ser", "org"))
    return jax.shard_map(
        per_device, mesh=mesh, in_specs=in_specs, out_specs=out_specs, check_vma=False
    )
```

```python
import functools

import jax
import jax.numpy as jnp
from jax import lax
from jax.experimental import pallas as pl
from jax.experimental.pallas import tpu as pltpu
from jax.sharding import PartitionSpec as P

SLOTS = 2048
TILE = 256
LANES = 128
ROWS = TILE // LANES
BLOCK = 64
OWNER_TILES = SLOTS // TILE
PANEL = 16
PIVOTS = 8

epsilon = 1e-06

NN = (((1,), (0,)), ((), ()))
NT = (((1,), (1,)), ((), ()))


def dot_bf16(left, right, dims=NN):
    return lax.dot_general(left, right, dims, preferred_element_type=jnp.float32)


def dot_f32(left, right, dims=NN):
    return lax.dot_general(
        left, right, dims, precision=lax.Precision.HIGHEST, preferred_element_type=jnp.float32
    )


def as_bf16(mask):
    return jnp.where(mask, 1.0, 0.0).astype(jnp.bfloat16)


def split_three(value):
    high = value.astype(jnp.bfloat16)
    rest = value - high.astype(jnp.float32)
    middle = rest.astype(jnp.bfloat16)
    low = (rest - middle.astype(jnp.float32)).astype(jnp.bfloat16)
    return jnp.concatenate([high, middle, low], axis=0)


def join_three(value):
    rows = value.shape[0] // 3
    return value[:rows] + value[rows : 2 * rows] + value[2 * rows :]


def iota(shape, dim):
    return lax.broadcasted_iota(jnp.int32, shape, dim)


def before_in_row(width):
    return as_bf16(iota((LANES, width), 0) < iota((LANES, width), 1))


def lane_pick(value, index):
    return jnp.take_along_axis(value, index, axis=1, mode="promise_in_bounds")


def scatter(entries, steps, groups):
    def add(g, total):
        key, value = entries(g)
        group = key >> 7
        lane = key & (LANES - 1)
        upper = (value >> 4).astype(jnp.float32)
        lower = (value & 15).astype(jnp.float32)
        lefts, rights = [], []
        for s in range(8):
            hit = iota((groups, LANES), 0) == group[s : s + 1]
            lefts.append(
                jnp.concatenate(
                    [jnp.where(hit, upper[s : s + 1], 0.0), jnp.where(hit, lower[s : s + 1], 0.0)],
                    axis=0,
                ).astype(jnp.bfloat16)
            )
            rights.append(as_bf16(iota((LANES, LANES), 0) == lane[s : s + 1]))
        return total + dot_bf16(
            jnp.concatenate(lefts, axis=1), jnp.concatenate(rights, axis=1), NT
        )

    start = jnp.zeros((2 * groups, LANES), jnp.float32)
    found = lax.fori_loop(0, steps, add, start, unroll=steps <= 8)
    return (found[:groups] * 16.0 + found[groups:]).astype(jnp.int32)


def take_columns(chunks, place):
    place = jnp.broadcast_to(place, (8, LANES))
    chunk = place >> 7
    lane = place & (LANES - 1)
    pieces = []
    for v in range(chunks[0].shape[0] // 8):
        taken = jnp.zeros((8, LANES), jnp.float32)
        for c, value in enumerate(chunks):
            taken = jnp.where(chunk == c, lane_pick(value[v * 8 : (v + 1) * 8], lane), taken)
        pieces.append(taken)
    return jnp.concatenate(pieces, axis=0)


def pack_body(
    size_hbm,
    owner_hbm,
    x_hbm,
    perm_hbm,
    send_hbm,
    place_ref,
    size_ref,
    owner_ref,
    x_ref,
    perm_ref,
    send_ref,
    in_sems,
    out_sems,
    *,
    n_ser,
    n_org,
):
    loads = [
        pltpu.make_async_copy(source, target, in_sems.at[i])
        for i, (source, target) in enumerate(
            [
                (size_hbm, size_ref),
                (owner_hbm, owner_ref),
                (perm_hbm, perm_ref),
                (x_hbm, x_ref),
            ]
        )
    ]
    for load in loads:
        load.start()
    here = lax.axis_index("ser")
    n_sub = size_ref.shape[0]
    rows = perm_ref.shape[0]
    t_dev, ser_dev = x_ref.shape
    per_peer = SLOTS // n_ser
    shift = ser_dev.bit_length() - 1
    for load in loads[:2]:
        load.wait()

    def owner_of(row_ids):
        owner = jnp.zeros(row_ids.shape, jnp.int32)
        start = jnp.int32(0)
        for k in range(n_sub):
            owner = jnp.where(row_ids >= start, owner_ref[k], owner)
            start = start + (size_ref[k] >> 7)
        return owner

    owner_down = owner_of(iota((rows, LANES), 0))
    owner_across = owner_of(iota((1, rows), 1))
    down_wide = owner_down[:, :rows] if rows <= LANES else owner_of(iota((rows, rows), 0))
    earlier = as_bf16(
        (down_wide == owner_across) & (iota((rows, rows), 1) < iota((rows, rows), 0))
    )
    loads[2].wait()
    mine = as_bf16((perm_ref[...] >> shift) == here)
    in_row = dot_bf16(mine, before_in_row(LANES))
    ahead = dot_bf16(earlier, mine).astype(jnp.bfloat16)
    in_rows = dot_bf16(ahead, jnp.ones((LANES, LANES), jnp.bfloat16))
    place_ref[...] = owner_down * per_peer + (in_row + in_rows).astype(jnp.int32)


    def entries(g):
        at = pl.ds(pl.multiple_of(g * 8, 8), 8)
        series = perm_ref[at, :]
        key = jnp.where((series >> shift) == here, place_ref[at, :], -1)
        return key, (series & (ser_dev - 1)) + 1

    column = scatter(entries, rows // 8, SLOTS // LANES) - 1
    loads[3].wait()
    chunks = [x_ref[:, c * LANES : (c + 1) * LANES] for c in range(ser_dev // LANES)]
    stores = [
        pltpu.make_async_copy(send_ref.at[o], send_hbm.at[o], out_sems.at[o])
        for o in range(n_ser)
    ]
    for k in range(SLOTS // LANES):
        taken = take_columns(chunks, column[k : k + 1])
        first = k * LANES // per_peer
        if per_peer >= LANES:
            start = k * LANES % per_peer
            send_ref[first, :, start : start + LANES] = taken
            if start + LANES == per_peer:
                stores[first].start()
        else:
            for h in range(LANES // per_peer):
                send_ref[first + h] = taken[:, h * per_peer : (h + 1) * per_peer]
                stores[first + h].start()
    for store in stores:
        store.wait()


def eliminate(parts, size, whole):
    lane = iota((8, LANES), 1)
    sub = iota((8, LANES), 0)
    base = lane & (LANES - size)
    local = lane & (size - 1)
    parts = [list(part) for part in parts]
    downs = [[jnp.ones((8, LANES), jnp.float32)] * len(part) for part in parts]
    acrosses = [jnp.ones((8, LANES), jnp.float32) for _ in parts]
    tall = PANEL // 8
    count = PIVOTS
    for top in range(0, size, PANEL):
        first = top // 8
        inside = (local >= top) & (local < top + PANEL)
        panels = [part[first : first + tall] for part in parts]
        kept = [list(panel) for panel in panels]
        for j in range(top, top + PANEL, count):
            g, s = divmod(j - top, 8)
            columns = [base + (j + a) for a in range(count)]
            at = [local == j + a for a in range(count)]
            on = (local >= j) & (local < j + count)
            for p, panel in enumerate(panels):
                picked = [[lane_pick(piece, column) for column in columns] for piece in panel]
                corner = [
                    [
                        jnp.broadcast_to(picked[g][b][s + a : s + a + 1], (8, LANES))
                        for b in range(a + 1)
                    ]
                    for a in range(count)
                ]
                inv, low = [], [[None] * count for _ in range(count)]
                for k in range(count):
                    inv.append(1.0 / corner[k][k])
                    for a in range(k + 1, count):
                        low[a][k] = corner[a][k] * inv[k]
                    for a in range(k + 1, count):
                        for b in range(k + 1, a + 1):
                            corner[a][b] = corner[a][b] - low[a][k] * corner[b][k]
                rows, solved = [], [None] * count
                for a in range(count):
                    row = jnp.broadcast_to(panel[g][s + a : s + a + 1], (8, LANES))
                    row = jnp.where(on, jnp.where(at[a], 1.0, 0.0), row)
                    for b in range(a):
                        row = row - low[a][b] * rows[b]
                    rows.append(row)
                for a in reversed(range(count)):
                    row = rows[a] * inv[a]
                    for b in range(a + 1, count):
                        row = row - low[b][a] * solved[b]
                    solved[a] = row
                for v in range(tall):
                    new = jnp.where(on, 0.0, panel[v])
                    for a in range(count):
                        new = new - picked[v][a] * solved[a]
                    if v == g:
                        for a in range(count):
                            new = jnp.where(sub == s + a, solved[a], new)
                    panel[v] = new
                if not whole:
                    for v in range(g, tall):
                        ahead = (sub >= s + count) | (v > g)
                        kept[p][v] = jnp.where(ahead, panel[v], kept[p][v])
                    for a in range(count):
                        here = sub == s + a
                        pivot = corner[a][a]
                        kept[p][g] = jnp.where(here, rows[a], kept[p][g])
                        downs[p][first + g] = jnp.where(here, pivot, downs[p][first + g])
                        acrosses[p] = jnp.where(at[a], pivot, acrosses[p])
        for p, part in enumerate(parts):
            others = [i for i in range(len(part)) if i >= first + tall or (whole and i < first)]
            if others:
                zero = jnp.zeros((8, LANES), jnp.float32)
                pieces = []
                for h in range(LANES // size):
                    half = base == h * size
                    for i in range(size // 8):
                        if first <= i < first + tall:
                            pieces.append(jnp.where(half, panels[p][i - first], 0.0))
                        else:
                            pieces.append(zero)
                change = dot_f32(
                    jnp.concatenate([part[i] for i in others], axis=0),
                    jnp.concatenate(pieces, axis=0),
                )
                for n, i in enumerate(others):
                    part[i] = jnp.where(inside, 0.0, part[i]) - change[n * 8 : n * 8 + 8]
            part[first : first + tall] = panels[p] if whole else kept[p]
    return parts, downs, acrosses


def slots_body(
    size_ref,
    owner_ref,
    perm_ref,
    place_ref,
    pick_ref,
    tile_of_ref,
    tile_ref,
    dest_ref,
    index_ref,
    *,
    n_ser,
    n_org,
    ser_dev,
):
    here = lax.axis_index("ser")
    part = lax.axis_index("org")
    n_sub = size_ref.shape[0]
    per_peer = SLOTS // n_ser
    share = SLOTS // n_org
    tiles = share // TILE
    shift = ser_dev.bit_length() - 1
    slot_rows = SLOTS // LANES
    wide = max(per_peer, LANES)

    def entries(g):
        at = pl.ds(pl.multiple_of(g * 8, 8), 8)
        series = perm_ref[at, :]
        return jnp.where((series >> shift) == here, series & (ser_dev - 1), -1), place_ref[at, :]

    dest_ref[...] = scatter(entries, perm_ref.shape[0] // 8, ser_dev // LANES)

    for t in range(OWNER_TILES):
        tile_ref[0, t] = jnp.int32(-1)
        tile_ref[1, t] = jnp.int32(0)
        tile_ref[2, t] = jnp.int32(0)
    at = jnp.int32(0)
    first = jnp.int32(0)
    for k in range(n_sub):
        count = size_ref[k] >> 8
        held = jnp.where(owner_ref[k] == here, count, 0)

        def put(i, carry, at=at, first=first, held=held):
            tile_ref[0, at + i] = first + i
            tile_ref[1, at + i] = at
            tile_ref[2, at + i] = at + held
            return carry

        lax.fori_loop(0, held, put, 0)
        at = at + held
        first = first + count

    pieces = []
    for t in range(OWNER_TILES):
        place = tile_ref[0, t]
        rows = perm_ref[pl.ds(jnp.maximum(place, 0) * ROWS, ROWS), :]
        pieces.append(jnp.where(place >= 0, rows, -1))
    source = jnp.concatenate(pieces, axis=0) >> shift
    from_peer = jnp.concatenate([as_bf16(source == d) for d in range(n_ser)], axis=0)
    in_row = dot_bf16(from_peer, before_in_row(LANES))
    row_total = dot_bf16(from_peer, jnp.ones((LANES, wide), jnp.bfloat16)).astype(jnp.bfloat16)
    span = n_ser * slot_rows
    left, right = iota((span, span), 0), iota((span, span), 1)
    ahead = as_bf16((left // slot_rows == right // slot_rows) & (right < left))
    base = dot_bf16(ahead, row_total)[:, :LANES]
    rank = jnp.zeros((slot_rows, LANES), jnp.float32)
    for d in range(n_ser):
        rows = slice(d * slot_rows, (d + 1) * slot_rows)
        rank = jnp.where(source == d, in_row[rows] + base[rows], rank)
    index_ref[...] = jnp.where(source >= 0, source * per_peer + rank.astype(jnp.int32), -1)
    left, right = iota((OWNER_TILES * n_ser, span), 0), iota((OWNER_TILES * n_ser, span), 1)
    through = as_bf16(
        (left % n_ser == right // slot_rows)
        & (right % slot_rows < ROWS * (left // n_ser) + ROWS)
    )
    ends = dot_bf16(through, row_total).astype(jnp.int32)[:, :per_peer]
    tile_of = jnp.zeros((n_ser, per_peer), jnp.int32)
    for t in range(OWNER_TILES):
        tile_of += (iota((n_ser, per_peer), 1) >= ends[t * n_ser : (t + 1) * n_ser]).astype(
            jnp.int32
        )
    tile_of = jnp.concatenate([tile_of[d : d + 1] for d in range(n_ser)], axis=1)
    tile_of_ref[...] = tile_of

    for i in range(share // LANES):
        row = index_ref[pl.ds(part * (tiles * ROWS) + i, 1), :]
        pick_ref[:, i * LANES : (i + 1) * LANES] = as_bf16(iota((SLOTS, LANES), 0) == row)


def owner_body(
    recv_ref,
    pick_ref,
    tile_of_ref,
    tile_ref,
    back_ref,
    log_ref,
    all_ref,
    inverse_ref,
    *,
    n_ser,
    n_org,
):
    part = lax.axis_index("org")
    t_dev = recv_ref.shape[1]
    anchors = t_dev * n_org
    per_peer = SLOTS // n_ser
    share = SLOTS // n_org
    tiles = share // TILE

    for d in range(n_ser):
        for r in range(n_org):
            all_ref[r * t_dev : (r + 1) * t_dev, d * per_peer : (d + 1) * per_peer] = recv_ref[
                r * n_ser + d
            ]

    tile_of = tile_of_ref[...]

    block = all_ref[...]
    spread = jnp.sum(block * block, axis=0, keepdims=True) * (1.0 / anchors)
    scaled = block * jnp.where(spread > 0, lax.rsqrt(spread), 0.0)
    own = spread / (spread + epsilon)
    fourth = jnp.sum(jnp.square(scaled * scaled), axis=0, keepdims=True) * (1.0 / anchors)
    in_tree, ahead_of, filled = [], [], []
    for u in range(tiles):
        t = part * tiles + u
        low, high = tile_ref[1, t], tile_ref[2, t]
        filled.append(tile_ref[0, t] >= 0)
        in_tree.append((tile_of >= low) & (tile_of < high))
        ahead_of.append((tile_of >= low) & (tile_of < t))
    terms = split_three(scaled)
    weighted = split_three(scaled * own)
    products = dot_bf16(
        jnp.concatenate(
            [weighted * as_bf16(mask) for mask in in_tree]
            + [terms * as_bf16(mask) for mask in ahead_of],
            axis=0,
        ),
        terms,
        NT,
    )
    grams = []
    for u in range(2 * tiles):
        piece = join_three(products[u * 3 * anchors : (u + 1) * 3 * anchors])
        grams.append(
            piece[:, 2 * anchors :] + piece[:, anchors : 2 * anchors] + piece[:, :anchors]
        )
    unit = iota((anchors, anchors), 0) == iota((anchors, anchors), 1)
    shrink = []
    for u in range(tiles):
        dual = grams[u] * (1.0 / anchors)
        own_square = jnp.where(in_tree[u], own * own, 0.0)
        square = dual * dual
        total = lambda value: jnp.sum(
            jnp.sum(value, axis=0, keepdims=True), axis=1, keepdims=True
        )
        lower = total(square) - total(own_square)
        upper = total(jnp.where(unit, square, 0.0)) * anchors - total(own_square * fourth)
        upper = (upper - lower) / (anchors - 1)
        shrink.append(jnp.where(filled[u], jnp.minimum(upper / jnp.where(filled[u], lower, 1.0), 1.0), 1.0))

    levels = split_three(jnp.broadcast_to(spread, (16, SLOTS)))
    found = dot_bf16(jnp.concatenate([terms, levels], axis=0), pick_ref[...])
    mine = join_three(found[: 3 * anchors])
    my_spread = join_three(found[3 * anchors :])[:1]
    mine_down = mine.T

    per_tile = TILE // BLOCK
    blocks = share // BLOCK
    side = LANES // anchors
    rows_of = lambda b: slice(b * BLOCK, (b + 1) * BLOCK)
    for u in range(tiles):
        prior = grams[tiles + u]
        gain = (1.0 - shrink[u]) * (1.0 / anchors)
        for v in range(per_tile):
            b = u * per_tile + v
            inverse_ref[b // side, :, (b % side) * anchors : (b % side + 1) * anchors] = (
                jnp.where(unit, shrink[u], 0.0) + gain * prior
            )
            if v < per_tile - 1:
                piece = mine[:, rows_of(b)]
                prior = prior + dot_f32(piece, piece, NT)

    inverses, _, _ = eliminate(
        [
            [inverse_ref[p, i * 8 : (i + 1) * 8, :] for i in range(anchors // 8)]
            for p in range(blocks // side)
        ],
        anchors,
        whole=True,
    )
    inverses = [jnp.concatenate(rows, axis=0) for rows in inverses]

    diagonal = iota((BLOCK, BLOCK), 0) == iota((BLOCK, BLOCK), 1)
    solved, weights = [], []
    for b in range(blocks):
        gain = (1.0 - shrink[b // per_tile]) * (1.0 / anchors)
        inverse = inverses[b // side][:, (b % side) * anchors : (b % side + 1) * anchors]
        solved.append(dot_f32(inverse, mine[:, rows_of(b)]))
        weights.append(
            jnp.where(diagonal, 1.0, 0.0) + gain * dot_f32(mine_down[rows_of(b)], solved[b])
        )
    pairs = [jnp.concatenate(weights[b : b + 2], axis=1) for b in range(0, blocks, 2)]
    lowers, downs, acrosses = eliminate(
        [[pair[i * 8 : (i + 1) * 8] for i in range(BLOCK // 8)] for pair in pairs],
        BLOCK,
        whole=False,
    )
    keep = iota((BLOCK, LANES), 0) >= (iota((BLOCK, LANES), 1) & (BLOCK - 1))
    done, logs = [], []
    for p in range(blocks // 2):
        lower = jnp.concatenate(
            [row * lax.rsqrt(pivot) for row, pivot in zip(lowers[p], downs[p])], axis=0
        )
        lower = jnp.where(keep, lower, 0.0)
        for h in range(2):
            b = 2 * p + h
            u = b // per_tile
            half = slice(h * BLOCK, (h + 1) * BLOCK)
            done.append(dot_f32(solved[b], lower[:, half], NT) * jnp.sqrt(shrink[u]))
            level = acrosses[p][:1, half] * my_spread[:, rows_of(b)] * shrink[u]
            logs.append(jnp.where(filled[u], 0.5 * jnp.log(level), 0.0))
    log_ref[...] = jnp.concatenate(logs, axis=1)
    terms = split_three(jnp.concatenate(done, axis=1))

    for d in range(n_ser):
        columns = join_three(
            dot_bf16(terms, pick_ref[d * per_peer : (d + 1) * per_peer, :], NT)
        )
        for r in range(n_org):
            back_ref[d * n_org + r] = columns[r * t_dev : (r + 1) * t_dev]


def home_body(back_ref, dest_ref, out_ref, *, n_ser, n_org):
    per_peer = back_ref.shape[2]
    pieces = []
    for o in range(n_ser):
        piece = back_ref[o * n_org]
        for q in range(1, n_org):
            piece = piece + back_ref[o * n_org + q]
        pieces.append(piece)
    whole = jnp.concatenate(pieces, axis=1)
    chunks = [whole[:, c * LANES : (c + 1) * LANES] for c in range(SLOTS // LANES)]
    for h in range(dest_ref.shape[0]):
        out_ref[:, h * LANES : (h + 1) * LANES] = take_columns(chunks, dest_ref[h : h + 1, :])


def per_device(residual, sub_size, sub_owner, series_perm):
    n_ser = lax.axis_size("ser")
    n_org = lax.axis_size("org")
    t_dev, ser_dev = residual.shape
    anchors = t_dev * n_org
    per_peer = SLOTS // n_ser
    share = SLOTS // n_org
    blocks = share // BLOCK
    side = LANES // anchors
    perm = series_perm.reshape(-1, LANES)
    to_hbm = lambda value: pltpu.with_memory_space_constraint(value, pltpu.HBM)
    vmem = pl.BlockSpec(memory_space=pltpu.VMEM)
    smem = pl.BlockSpec(memory_space=pltpu.SMEM)
    hbm = pl.BlockSpec(memory_space=pltpu.HBM)
    params = pltpu.CompilerParams(vmem_limit_bytes=48 * 1024 * 1024)
    blocks_shape = jax.ShapeDtypeStruct((n_ser * n_org, t_dev, per_peer), jnp.float32)

    send, place = pl.pallas_call(
        functools.partial(pack_body, n_ser=n_ser, n_org=n_org),
        out_shape=(jax.ShapeDtypeStruct((n_ser, t_dev, per_peer), jnp.float32), jax.ShapeDtypeStruct(perm.shape, jnp.int32)),
        in_specs=[hbm, hbm, hbm, hbm],
        out_specs=(hbm, vmem),
        scratch_shapes=[
            pltpu.SMEM(sub_size.shape, jnp.int32),
            pltpu.SMEM(sub_owner.shape, jnp.int32),
            pltpu.VMEM(residual.shape, jnp.float32),
            pltpu.VMEM(perm.shape, jnp.int32),
            pltpu.VMEM((n_ser, t_dev, per_peer), jnp.float32),
            pltpu.SemaphoreType.DMA((4,)),
            pltpu.SemaphoreType.DMA((n_ser,)),
        ],
        compiler_params=params,
        name="pack",
    )(to_hbm(sub_size), to_hbm(sub_owner), to_hbm(residual), to_hbm(perm))
    recv = lax.all_to_all(send, "ser", split_axis=0, concat_axis=0, tiled=True)
    recv = lax.all_gather(recv, "org", axis=0, tiled=True)
    pick, tile_of, tile, dest = pl.pallas_call(
        functools.partial(slots_body, n_ser=n_ser, n_org=n_org, ser_dev=ser_dev),
        out_shape=(
            jax.ShapeDtypeStruct((SLOTS, share), jnp.bfloat16),
            jax.ShapeDtypeStruct((1, SLOTS), jnp.int32),
            jax.ShapeDtypeStruct((3, OWNER_TILES), jnp.int32),
            jax.ShapeDtypeStruct((ser_dev // LANES, LANES), jnp.int32),
        ),
        in_specs=[smem, smem, vmem, vmem],
        out_specs=(vmem, vmem, smem, vmem),
        scratch_shapes=[pltpu.VMEM((SLOTS // LANES, LANES), jnp.int32)],
        compiler_params=params,
        cost_estimate=pl.CostEstimate(
            flops=4_000_000_000, bytes_accessed=4_000_000, transcendentals=0
        ),
        name="slots",
    )(sub_size, sub_owner, perm, place)
    back, log_part = pl.pallas_call(
        functools.partial(owner_body, n_ser=n_ser, n_org=n_org),
        out_shape=(blocks_shape, jax.ShapeDtypeStruct((1, share), jnp.float32)),
        in_specs=[vmem, vmem, vmem, smem],
        out_specs=(vmem, vmem),
        scratch_shapes=[
            pltpu.VMEM((anchors, SLOTS), jnp.float32),
            pltpu.VMEM((blocks // side, anchors, LANES), jnp.float32),
        ],
        compiler_params=params,
        name="owner",
    )(recv, pick, tile_of, tile)
    returned = lax.all_to_all(back, ("ser", "org"), split_axis=0, concat_axis=0, tiled=True)
    whitened = pl.pallas_call(
        functools.partial(home_body, n_ser=n_ser, n_org=n_org),
        out_shape=jax.ShapeDtypeStruct((t_dev, ser_dev), jnp.float32),
        in_specs=[vmem, vmem],
        out_specs=vmem,
        compiler_params=params,
        name="home",
    )(returned, dest)
    return (whitened, log_part)


def solution(mesh):
    in_specs = (P("org", "ser"), P(), P(), P())
    out_specs = (P("org", "ser"), P("ser", "org"))
    return jax.shard_map(
        per_device, mesh=mesh, in_specs=in_specs, out_specs=out_specs, check_vma=False
    )
```

```python
import functools

import jax
import jax.numpy as jnp
from jax import lax
from jax.experimental import pallas as pl
from jax.experimental.pallas import tpu as pltpu
from jax.sharding import PartitionSpec as P

SLOTS = 2048
TILE = 256
LANES = 128
ROWS = TILE // LANES
BLOCK = 64
OWNER_TILES = SLOTS // TILE
PANEL = 16
PIVOTS = 8

epsilon = 1e-06

NN = (((1,), (0,)), ((), ()))
NT = (((1,), (1,)), ((), ()))


def dot_bf16(left, right, dims=NN):
    return lax.dot_general(left, right, dims, preferred_element_type=jnp.float32)


def dot_f32(left, right, dims=NN):
    return lax.dot_general(
        left, right, dims, precision=lax.Precision.HIGHEST, preferred_element_type=jnp.float32
    )


def as_bf16(mask):
    return jnp.where(mask, 1.0, 0.0).astype(jnp.bfloat16)


def split_three(value):
    high = value.astype(jnp.bfloat16)
    rest = value - high.astype(jnp.float32)
    middle = rest.astype(jnp.bfloat16)
    low = (rest - middle.astype(jnp.float32)).astype(jnp.bfloat16)
    return jnp.concatenate([high, middle, low], axis=0)


def join_three(value):
    rows = value.shape[0] // 3
    return value[:rows] + value[rows : 2 * rows] + value[2 * rows :]


def iota(shape, dim):
    return lax.broadcasted_iota(jnp.int32, shape, dim)


def before_in_row(width):
    return as_bf16(iota((LANES, width), 0) < iota((LANES, width), 1))


def lane_pick(value, index):
    return jnp.take_along_axis(value, index, axis=1, mode="promise_in_bounds")


def scatter(entries, steps, groups):
    def add(g, total):
        key, value = entries(g)
        group = key >> 7
        lane = key & (LANES - 1)
        upper = (value >> 4).astype(jnp.float32)
        lower = (value & 15).astype(jnp.float32)
        lefts, rights = [], []
        for s in range(8):
            hit = iota((groups, LANES), 0) == group[s : s + 1]
            lefts.append(
                jnp.concatenate(
                    [jnp.where(hit, upper[s : s + 1], 0.0), jnp.where(hit, lower[s : s + 1], 0.0)],
                    axis=0,
                ).astype(jnp.bfloat16)
            )
            rights.append(as_bf16(iota((LANES, LANES), 0) == lane[s : s + 1]))
        return total + dot_bf16(
            jnp.concatenate(lefts, axis=1), jnp.concatenate(rights, axis=1), NT
        )

    start = jnp.zeros((2 * groups, LANES), jnp.float32)
    found = lax.fori_loop(0, steps, add, start, unroll=steps <= 8)
    return (found[:groups] * 16.0 + found[groups:]).astype(jnp.int32)


def take_columns(chunks, place):
    place = jnp.broadcast_to(place, (8, LANES))
    chunk = place >> 7
    lane = place & (LANES - 1)
    pieces = []
    for v in range(chunks[0].shape[0] // 8):
        taken = jnp.zeros((8, LANES), jnp.float32)
        for c, value in enumerate(chunks):
            taken = jnp.where(chunk == c, lane_pick(value[v * 8 : (v + 1) * 8], lane), taken)
        pieces.append(taken)
    return jnp.concatenate(pieces, axis=0)


def pack_body(
    size_hbm,
    owner_hbm,
    x_hbm,
    perm_hbm,
    send_hbm,
    place_ref,
    size_ref,
    owner_ref,
    x_ref,
    perm_ref,
    send_ref,
    in_sems,
    out_sems,
    *,
    n_ser,
    n_org,
):
    loads = [
        pltpu.make_async_copy(source, target, in_sems.at[i])
        for i, (source, target) in enumerate(
            [
                (size_hbm, size_ref),
                (owner_hbm, owner_ref),
                (perm_hbm, perm_ref),
                (x_hbm, x_ref),
            ]
        )
    ]
    for load in loads:
        load.start()
    here = lax.axis_index("ser")
    n_sub = size_ref.shape[0]
    rows = perm_ref.shape[0]
    t_dev, ser_dev = x_ref.shape
    per_peer = SLOTS // n_ser
    shift = ser_dev.bit_length() - 1
    for load in loads[:2]:
        load.wait()

    def owner_of(row_ids):
        owner = jnp.zeros(row_ids.shape, jnp.int32)
        start = jnp.int32(0)
        for k in range(n_sub):
            owner = jnp.where(row_ids >= start, owner_ref[k], owner)
            start = start + (size_ref[k] >> 7)
        return owner

    owner_down = owner_of(iota((rows, LANES), 0))
    owner_across = owner_of(iota((1, rows), 1))
    down_wide = owner_down[:, :rows] if rows <= LANES else owner_of(iota((rows, rows), 0))
    earlier = as_bf16(
        (down_wide == owner_across) & (iota((rows, rows), 1) < iota((rows, rows), 0))
    )
    loads[2].wait()
    mine = as_bf16((perm_ref[...] >> shift) == here)
    in_row = dot_bf16(mine, before_in_row(LANES))
    ahead = dot_bf16(earlier, mine).astype(jnp.bfloat16)
    in_rows = dot_bf16(ahead, jnp.ones((LANES, LANES), jnp.bfloat16))
    place_ref[...] = owner_down * per_peer + (in_row + in_rows).astype(jnp.int32)


    def entries(g):
        at = pl.ds(pl.multiple_of(g * 8, 8), 8)
        series = perm_ref[at, :]
        key = jnp.where((series >> shift) == here, place_ref[at, :], -1)
        return key, (series & (ser_dev - 1)) + 1

    column = scatter(entries, rows // 8, SLOTS // LANES) - 1
    loads[3].wait()
    chunks = [x_ref[:, c * LANES : (c + 1) * LANES] for c in range(ser_dev // LANES)]
    stores = [
        pltpu.make_async_copy(send_ref.at[o], send_hbm.at[o], out_sems.at[o])
        for o in range(n_ser)
    ]
    for k in range(SLOTS // LANES):
        taken = take_columns(chunks, column[k : k + 1])
        first = k * LANES // per_peer
        if per_peer >= LANES:
            start = k * LANES % per_peer
            send_ref[first, :, start : start + LANES] = taken
            if start + LANES == per_peer:
                stores[first].start()
        else:
            for h in range(LANES // per_peer):
                send_ref[first + h] = taken[:, h * per_peer : (h + 1) * per_peer]
                stores[first + h].start()
    for store in stores:
        store.wait()


def eliminate(parts, size, whole):
    lane = iota((8, LANES), 1)
    sub = iota((8, LANES), 0)
    base = lane & (LANES - size)
    local = lane & (size - 1)
    parts = [list(part) for part in parts]
    downs = [[jnp.ones((8, LANES), jnp.float32)] * len(part) for part in parts]
    acrosses = [jnp.ones((8, LANES), jnp.float32) for _ in parts]
    tall = PANEL // 8
    count = PIVOTS
    for top in range(0, size, PANEL):
        first = top // 8
        inside = (local >= top) & (local < top + PANEL)
        panels = [part[first : first + tall] for part in parts]
        kept = [list(panel) for panel in panels]
        for j in range(top, top + PANEL, count):
            g, s = divmod(j - top, 8)
            columns = [base + (j + a) for a in range(count)]
            at = [local == j + a for a in range(count)]
            on = (local >= j) & (local < j + count)
            for p, panel in enumerate(panels):
                picked = [[lane_pick(piece, column) for column in columns] for piece in panel]
                corner = [
                    [
                        jnp.broadcast_to(picked[g][b][s + a : s + a + 1], (8, LANES))
                        for b in range(a + 1)
                    ]
                    for a in range(count)
                ]
                inv, low = [], [[None] * count for _ in range(count)]
                for k in range(count):
                    inv.append(1.0 / corner[k][k])
                    for a in range(k + 1, count):
                        low[a][k] = corner[a][k] * inv[k]
                    for a in range(k + 1, count):
                        for b in range(k + 1, a + 1):
                            corner[a][b] = corner[a][b] - low[a][k] * corner[b][k]
                rows, solved = [], [None] * count
                for a in range(count):
                    row = jnp.broadcast_to(panel[g][s + a : s + a + 1], (8, LANES))
                    row = jnp.where(on, jnp.where(at[a], 1.0, 0.0), row)
                    for b in range(a):
                        row = row - low[a][b] * rows[b]
                    rows.append(row)
                for a in reversed(range(count)):
                    row = rows[a] * inv[a]
                    for b in reversed(range(a + 1, count)):
                        row = row - low[b][a] * solved[b]
                    solved[a] = row
                for v in range(tall):
                    new = jnp.where(on, 0.0, panel[v])
                    for a in reversed(range(count)):
                        new = new - picked[v][a] * solved[a]
                    if v == g:
                        for a in range(count):
                            new = jnp.where(sub == s + a, solved[a], new)
                    panel[v] = new
                if not whole:
                    for v in range(g, tall):
                        ahead = (sub >= s + count) | (v > g)
                        kept[p][v] = jnp.where(ahead, panel[v], kept[p][v])
                    for a in range(count):
                        here = sub == s + a
                        pivot = corner[a][a]
                        kept[p][g] = jnp.where(here, rows[a], kept[p][g])
                        downs[p][first + g] = jnp.where(here, pivot, downs[p][first + g])
                        acrosses[p] = jnp.where(at[a], pivot, acrosses[p])
        for p, part in enumerate(parts):
            others = [i for i in range(len(part)) if i >= first + tall or (whole and i < first)]
            if others:
                zero = jnp.zeros((8, LANES), jnp.float32)
                pieces = []
                for h in range(LANES // size):
                    half = base == h * size
                    for i in range(size // 8):
                        if first <= i < first + tall:
                            pieces.append(jnp.where(half, panels[p][i - first], 0.0))
                        else:
                            pieces.append(zero)
                change = dot_f32(
                    jnp.concatenate([part[i] for i in others], axis=0),
                    jnp.concatenate(pieces, axis=0),
                )
                for n, i in enumerate(others):
                    part[i] = jnp.where(inside, 0.0, part[i]) - change[n * 8 : n * 8 + 8]
            part[first : first + tall] = panels[p] if whole else kept[p]
    return parts, downs, acrosses


def slots_body(
    size_ref,
    owner_ref,
    perm_ref,
    place_ref,
    pick_ref,
    tile_of_ref,
    tile_ref,
    dest_ref,
    index_ref,
    *,
    n_ser,
    n_org,
    ser_dev,
):
    here = lax.axis_index("ser")
    part = lax.axis_index("org")
    n_sub = size_ref.shape[0]
    per_peer = SLOTS // n_ser
    share = SLOTS // n_org
    tiles = share // TILE
    shift = ser_dev.bit_length() - 1
    slot_rows = SLOTS // LANES
    wide = max(per_peer, LANES)

    def entries(g):
        at = pl.ds(pl.multiple_of(g * 8, 8), 8)
        series = perm_ref[at, :]
        return jnp.where((series >> shift) == here, series & (ser_dev - 1), -1), place_ref[at, :]

    dest_ref[...] = scatter(entries, perm_ref.shape[0] // 8, ser_dev // LANES)

    for t in range(OWNER_TILES):
        tile_ref[0, t] = jnp.int32(-1)
        tile_ref[1, t] = jnp.int32(0)
        tile_ref[2, t] = jnp.int32(0)
    at = jnp.int32(0)
    first = jnp.int32(0)
    for k in range(n_sub):
        count = size_ref[k] >> 8
        held = jnp.where(owner_ref[k] == here, count, 0)

        def put(i, carry, at=at, first=first, held=held):
            tile_ref[0, at + i] = first + i
            tile_ref[1, at + i] = at
            tile_ref[2, at + i] = at + held
            return carry

        lax.fori_loop(0, held, put, 0)
        at = at + held
        first = first + count

    pieces = []
    for t in range(OWNER_TILES):
        place = tile_ref[0, t]
        rows = perm_ref[pl.ds(jnp.maximum(place, 0) * ROWS, ROWS), :]
        pieces.append(jnp.where(place >= 0, rows, -1))
    source = jnp.concatenate(pieces, axis=0) >> shift
    from_peer = jnp.concatenate([as_bf16(source == d) for d in range(n_ser)], axis=0)
    in_row = dot_bf16(from_peer, before_in_row(LANES))
    row_total = dot_bf16(from_peer, jnp.ones((LANES, wide), jnp.bfloat16)).astype(jnp.bfloat16)
    span = n_ser * slot_rows
    left, right = iota((span, span), 0), iota((span, span), 1)
    ahead = as_bf16((left // slot_rows == right // slot_rows) & (right < left))
    base = dot_bf16(ahead, row_total)[:, :LANES]
    rank = jnp.zeros((slot_rows, LANES), jnp.float32)
    for d in range(n_ser):
        rows = slice(d * slot_rows, (d + 1) * slot_rows)
        rank = jnp.where(source == d, in_row[rows] + base[rows], rank)
    index_ref[...] = jnp.where(source >= 0, source * per_peer + rank.astype(jnp.int32), -1)
    left, right = iota((OWNER_TILES * n_ser, span), 0), iota((OWNER_TILES * n_ser, span), 1)
    through = as_bf16(
        (left % n_ser == right // slot_rows)
        & (right % slot_rows < ROWS * (left // n_ser) + ROWS)
    )
    ends = dot_bf16(through, row_total).astype(jnp.int32)[:, :per_peer]
    tile_of = jnp.zeros((n_ser, per_peer), jnp.int32)
    for t in range(OWNER_TILES):
        tile_of += (iota((n_ser, per_peer), 1) >= ends[t * n_ser : (t + 1) * n_ser]).astype(
            jnp.int32
        )
    tile_of = jnp.concatenate([tile_of[d : d + 1] for d in range(n_ser)], axis=1)
    tile_of_ref[...] = tile_of

    for i in range(share // LANES):
        row = index_ref[pl.ds(part * (tiles * ROWS) + i, 1), :]
        pick_ref[:, i * LANES : (i + 1) * LANES] = as_bf16(iota((SLOTS, LANES), 0) == row)


def owner_body(*refs, n_ser, n_org, flips):
    recv_refs = refs[:n_org]
    pick_ref, tile_of_ref, tile_ref, back_ref, log_ref, all_ref, inverse_ref = refs[n_org:]
    part = lax.axis_index("org")
    t_dev = recv_refs[0].shape[1]
    anchors = t_dev * n_org
    per_peer = SLOTS // n_ser
    share = SLOTS // n_org
    tiles = share // TILE

    for flip, part_ref in zip(flips, recv_refs):
        row = pl.multiple_of((part ^ flip) * t_dev, t_dev)
        for d in range(n_ser):
            all_ref[pl.ds(row, t_dev), d * per_peer : (d + 1) * per_peer] = part_ref[d]

    tile_of = tile_of_ref[...]

    block = all_ref[...]
    spread = jnp.sum(block * block, axis=0, keepdims=True) * (1.0 / anchors)
    scaled = block * jnp.where(spread > 0, lax.rsqrt(spread), 0.0)
    own = spread / (spread + epsilon)
    fourth = jnp.sum(jnp.square(scaled * scaled), axis=0, keepdims=True) * (1.0 / anchors)
    in_tree, ahead_of, filled = [], [], []
    for u in range(tiles):
        t = part * tiles + u
        low, high = tile_ref[1, t], tile_ref[2, t]
        filled.append(tile_ref[0, t] >= 0)
        in_tree.append((tile_of >= low) & (tile_of < high))
        ahead_of.append((tile_of >= low) & (tile_of < t))
    terms = split_three(scaled)
    weighted = split_three(scaled * own)
    products = dot_bf16(
        jnp.concatenate(
            [weighted * as_bf16(mask) for mask in in_tree]
            + [terms * as_bf16(mask) for mask in ahead_of],
            axis=0,
        ),
        terms,
        NT,
    )
    grams = []
    for u in range(2 * tiles):
        piece = join_three(products[u * 3 * anchors : (u + 1) * 3 * anchors])
        grams.append(
            piece[:, 2 * anchors :] + piece[:, anchors : 2 * anchors] + piece[:, :anchors]
        )
    unit = iota((anchors, anchors), 0) == iota((anchors, anchors), 1)
    shrink = []
    for u in range(tiles):
        dual = grams[u] * (1.0 / anchors)
        own_square = jnp.where(in_tree[u], own * own, 0.0)
        square = dual * dual
        total = lambda value: jnp.sum(
            jnp.sum(value, axis=0, keepdims=True), axis=1, keepdims=True
        )
        lower = total(square) - total(own_square)
        upper = total(jnp.where(unit, square, 0.0)) * anchors - total(own_square * fourth)
        upper = (upper - lower) / (anchors - 1)
        shrink.append(jnp.where(filled[u], jnp.minimum(upper / jnp.where(filled[u], lower, 1.0), 1.0), 1.0))

    levels = split_three(jnp.broadcast_to(spread, (16, SLOTS)))
    found = dot_bf16(jnp.concatenate([terms, levels], axis=0), pick_ref[...])
    mine = join_three(found[: 3 * anchors])
    my_spread = join_three(found[3 * anchors :])[:1]
    mine_down = mine.T

    per_tile = TILE // BLOCK
    blocks = share // BLOCK
    side = LANES // anchors
    rows_of = lambda b: slice(b * BLOCK, (b + 1) * BLOCK)
    for u in range(tiles):
        prior = grams[tiles + u]
        gain = (1.0 - shrink[u]) * (1.0 / anchors)
        for v in range(per_tile):
            b = u * per_tile + v
            inverse_ref[b // side, :, (b % side) * anchors : (b % side + 1) * anchors] = (
                jnp.where(unit, shrink[u], 0.0) + gain * prior
            )
            if v < per_tile - 1:
                piece = mine[:, rows_of(b)]
                prior = prior + dot_f32(piece, piece, NT)

    inverses, _, _ = eliminate(
        [
            [inverse_ref[p, i * 8 : (i + 1) * 8, :] for i in range(anchors // 8)]
            for p in range(blocks // side)
        ],
        anchors,
        whole=True,
    )
    inverses = [jnp.concatenate(rows, axis=0) for rows in inverses]

    diagonal = iota((BLOCK, BLOCK), 0) == iota((BLOCK, BLOCK), 1)
    solved, weights = [], []
    for b in range(blocks):
        gain = (1.0 - shrink[b // per_tile]) * (1.0 / anchors)
        inverse = inverses[b // side][:, (b % side) * anchors : (b % side + 1) * anchors]
        solved.append(dot_f32(inverse, mine[:, rows_of(b)]))
        weights.append(
            jnp.where(diagonal, 1.0, 0.0) + gain * dot_f32(mine_down[rows_of(b)], solved[b])
        )
    pairs = [jnp.concatenate(weights[b : b + 2], axis=1) for b in range(0, blocks, 2)]
    lowers, downs, acrosses = eliminate(
        [[pair[i * 8 : (i + 1) * 8] for i in range(BLOCK // 8)] for pair in pairs],
        BLOCK,
        whole=False,
    )
    keep = iota((BLOCK, LANES), 0) >= (iota((BLOCK, LANES), 1) & (BLOCK - 1))
    done, logs = [], []
    for p in range(blocks // 2):
        lower = jnp.concatenate(
            [row * lax.rsqrt(pivot) for row, pivot in zip(lowers[p], downs[p])], axis=0
        )
        lower = jnp.where(keep, lower, 0.0)
        for h in range(2):
            b = 2 * p + h
            u = b // per_tile
            half = slice(h * BLOCK, (h + 1) * BLOCK)
            done.append(dot_f32(solved[b], lower[:, half], NT) * jnp.sqrt(shrink[u]))
            level = acrosses[p][:1, half] * my_spread[:, rows_of(b)] * shrink[u]
            logs.append(jnp.where(filled[u], 0.5 * jnp.log(level), 0.0))
    log_ref[...] = jnp.concatenate(logs, axis=1)
    terms = split_three(jnp.concatenate(done, axis=1))

    for d in range(n_ser):
        columns = join_three(
            dot_bf16(terms, pick_ref[d * per_peer : (d + 1) * per_peer, :], NT)
        )
        for r in range(n_org):
            back_ref[d * n_org + r] = columns[r * t_dev : (r + 1) * t_dev]


def home_body(back_ref, dest_ref, out_ref, *, n_ser, n_org):
    per_peer = back_ref.shape[2]
    pieces = []
    for o in range(n_ser):
        piece = back_ref[o * n_org]
        for q in range(1, n_org):
            piece = piece + back_ref[o * n_org + q]
        pieces.append(piece)
    whole = jnp.concatenate(pieces, axis=1)
    chunks = [whole[:, c * LANES : (c + 1) * LANES] for c in range(SLOTS // LANES)]
    for h in range(dest_ref.shape[0]):
        out_ref[:, h * LANES : (h + 1) * LANES] = take_columns(chunks, dest_ref[h : h + 1, :])


def per_device(residual, sub_size, sub_owner, series_perm):
    n_ser = lax.axis_size("ser")
    n_org = lax.axis_size("org")
    t_dev, ser_dev = residual.shape
    anchors = t_dev * n_org
    per_peer = SLOTS // n_ser
    share = SLOTS // n_org
    blocks = share // BLOCK
    side = LANES // anchors
    perm = series_perm.reshape(-1, LANES)
    to_hbm = lambda value: pltpu.with_memory_space_constraint(value, pltpu.HBM)
    vmem = pl.BlockSpec(memory_space=pltpu.VMEM)
    smem = pl.BlockSpec(memory_space=pltpu.SMEM)
    hbm = pl.BlockSpec(memory_space=pltpu.HBM)
    params = pltpu.CompilerParams(vmem_limit_bytes=48 * 1024 * 1024)
    blocks_shape = jax.ShapeDtypeStruct((n_ser * n_org, t_dev, per_peer), jnp.float32)

    send, place = pl.pallas_call(
        functools.partial(pack_body, n_ser=n_ser, n_org=n_org),
        out_shape=(jax.ShapeDtypeStruct((n_ser, t_dev, per_peer), jnp.float32), jax.ShapeDtypeStruct(perm.shape, jnp.int32)),
        in_specs=[hbm, hbm, hbm, hbm],
        out_specs=(hbm, vmem),
        scratch_shapes=[
            pltpu.SMEM(sub_size.shape, jnp.int32),
            pltpu.SMEM(sub_owner.shape, jnp.int32),
            pltpu.VMEM(residual.shape, jnp.float32),
            pltpu.VMEM(perm.shape, jnp.int32),
            pltpu.VMEM((n_ser, t_dev, per_peer), jnp.float32),
            pltpu.SemaphoreType.DMA((4,)),
            pltpu.SemaphoreType.DMA((n_ser,)),
        ],
        compiler_params=params,
        name="pack",
    )(to_hbm(sub_size), to_hbm(sub_owner), to_hbm(residual), to_hbm(perm))
    recv = lax.all_to_all(send, "ser", split_axis=0, concat_axis=0, tiled=True)
    pick, tile_of, tile, dest = pl.pallas_call(
        functools.partial(slots_body, n_ser=n_ser, n_org=n_org, ser_dev=ser_dev),
        out_shape=(
            jax.ShapeDtypeStruct((SLOTS, share), jnp.bfloat16),
            jax.ShapeDtypeStruct((1, SLOTS), jnp.int32),
            jax.ShapeDtypeStruct((3, OWNER_TILES), jnp.int32),
            jax.ShapeDtypeStruct((ser_dev // LANES, LANES), jnp.int32),
        ),
        in_specs=[smem, smem, vmem, vmem],
        out_specs=(vmem, vmem, smem, vmem),
        scratch_shapes=[pltpu.VMEM((SLOTS // LANES, LANES), jnp.int32)],
        compiler_params=params,
        cost_estimate=pl.CostEstimate(
            flops=4_000_000_000, bytes_accessed=4_000_000, transcendentals=0
        ),
        name="slots",
    )(sub_size, sub_owner, perm, place)
    recv, pick, tile_of, tile, dest = lax.optimization_barrier(
        (recv, pick, tile_of, tile, dest)
    )
    received, flips, bit = [recv], [0], n_org // 2
    while bit:
        swap = [(i, i ^ bit) for i in range(n_org)]
        received = received + [lax.ppermute(part, "org", swap) for part in received]
        flips = flips + [flip ^ bit for flip in flips]
        bit //= 2
    back, log_part = pl.pallas_call(
        functools.partial(owner_body, n_ser=n_ser, n_org=n_org, flips=flips),
        out_shape=(blocks_shape, jax.ShapeDtypeStruct((1, share), jnp.float32)),
        in_specs=[vmem] * n_org + [vmem, vmem, smem],
        out_specs=(vmem, vmem),
        scratch_shapes=[
            pltpu.VMEM((anchors, SLOTS), jnp.float32),
            pltpu.VMEM((blocks // side, anchors, LANES), jnp.float32),
        ],
        compiler_params=params,
        name="owner",
    )(*received, pick, tile_of, tile)
    returned = lax.all_to_all(back, ("ser", "org"), split_axis=0, concat_axis=0, tiled=True)
    whitened = pl.pallas_call(
        functools.partial(home_body, n_ser=n_ser, n_org=n_org),
        out_shape=jax.ShapeDtypeStruct((t_dev, ser_dev), jnp.float32),
        in_specs=[vmem, vmem],
        out_specs=vmem,
        compiler_params=params,
        name="home",
    )(returned, dest)
    return (whitened, log_part)


def solution(mesh):
    in_specs = (P("org", "ser"), P(), P(), P())
    out_specs = (P("org", "ser"), P("ser", "org"))
    return jax.shard_map(
        per_device, mesh=mesh, in_specs=in_specs, out_specs=out_specs, check_vma=False
    )
```

```python
import functools

import jax
import jax.numpy as jnp
from jax import lax
from jax.experimental import pallas as pl
from jax.experimental.pallas import tpu as pltpu
from jax.sharding import PartitionSpec as P

SLOTS = 2048
TILE = 256
LANES = 128
ROWS = TILE // LANES
BLOCK = 64
OWNER_TILES = SLOTS // TILE
PANEL = 16
PIVOTS = 8

epsilon = 1e-06

NN = (((1,), (0,)), ((), ()))
NT = (((1,), (1,)), ((), ()))


def dot_bf16(left, right, dims=NN):
    return lax.dot_general(left, right, dims, preferred_element_type=jnp.float32)


def dot_f32(left, right, dims=NN):
    return lax.dot_general(
        left, right, dims, precision=lax.Precision.HIGHEST, preferred_element_type=jnp.float32
    )


def as_bf16(mask):
    return jnp.where(mask, 1.0, 0.0).astype(jnp.bfloat16)


def split_three(value):
    high = value.astype(jnp.bfloat16)
    rest = value - high.astype(jnp.float32)
    middle = rest.astype(jnp.bfloat16)
    low = (rest - middle.astype(jnp.float32)).astype(jnp.bfloat16)
    return jnp.concatenate([high, middle, low], axis=0)


def join_three(value):
    rows = value.shape[0] // 3
    return value[:rows] + value[rows : 2 * rows] + value[2 * rows :]


def iota(shape, dim):
    return lax.broadcasted_iota(jnp.int32, shape, dim)


def before_in_row(width):
    return as_bf16(iota((LANES, width), 0) < iota((LANES, width), 1))


def lane_pick(value, index):
    return jnp.take_along_axis(value, index, axis=1, mode="promise_in_bounds")


def scatter(entries, steps, groups):
    def add(g, total):
        key, value = entries(g)
        group = key >> 7
        lane = key & (LANES - 1)
        upper = (value >> 4).astype(jnp.float32)
        lower = (value & 15).astype(jnp.float32)
        lefts, rights = [], []
        for s in range(8):
            hit = iota((groups, LANES), 0) == group[s : s + 1]
            lefts.append(
                jnp.concatenate(
                    [jnp.where(hit, upper[s : s + 1], 0.0), jnp.where(hit, lower[s : s + 1], 0.0)],
                    axis=0,
                ).astype(jnp.bfloat16)
            )
            rights.append(as_bf16(iota((LANES, LANES), 0) == lane[s : s + 1]))
        return total + dot_bf16(
            jnp.concatenate(lefts, axis=1), jnp.concatenate(rights, axis=1), NT
        )

    start = jnp.zeros((2 * groups, LANES), jnp.float32)
    found = lax.fori_loop(0, steps, add, start, unroll=steps <= 8)
    return (found[:groups] * 16.0 + found[groups:]).astype(jnp.int32)


def take_columns(chunks, place):
    place = jnp.broadcast_to(place, (8, LANES))
    chunk = place >> 7
    lane = place & (LANES - 1)
    pieces = []
    for v in range(chunks[0].shape[0] // 8):
        taken = jnp.zeros((8, LANES), jnp.float32)
        for c, value in enumerate(chunks):
            taken = jnp.where(chunk == c, lane_pick(value[v * 8 : (v + 1) * 8], lane), taken)
        pieces.append(taken)
    return jnp.concatenate(pieces, axis=0)


def pack_body(
    size_hbm,
    owner_hbm,
    x_hbm,
    perm_hbm,
    send_hbm,
    place_ref,
    size_ref,
    owner_ref,
    x_ref,
    perm_ref,
    send_ref,
    in_sems,
    out_sems,
    *,
    n_ser,
    n_org,
):
    loads = [
        pltpu.make_async_copy(source, target, in_sems.at[i])
        for i, (source, target) in enumerate(
            [
                (size_hbm, size_ref),
                (owner_hbm, owner_ref),
                (perm_hbm, perm_ref),
                (x_hbm, x_ref),
            ]
        )
    ]
    for load in loads:
        load.start()
    here = lax.axis_index("ser")
    n_sub = size_ref.shape[0]
    rows = perm_ref.shape[0]
    t_dev, ser_dev = x_ref.shape
    per_peer = SLOTS // n_ser
    shift = ser_dev.bit_length() - 1
    for load in loads[:2]:
        load.wait()

    def owner_of(row_ids):
        owner = jnp.zeros(row_ids.shape, jnp.int32)
        start = jnp.int32(0)
        for k in range(n_sub):
            owner = jnp.where(row_ids >= start, owner_ref[k], owner)
            start = start + (size_ref[k] >> 7)
        return owner

    owner_down = owner_of(iota((rows, LANES), 0))
    owner_across = owner_of(iota((1, rows), 1))
    down_wide = owner_down[:, :rows] if rows <= LANES else owner_of(iota((rows, rows), 0))
    earlier = as_bf16(
        (down_wide == owner_across) & (iota((rows, rows), 1) < iota((rows, rows), 0))
    )
    loads[2].wait()
    mine = as_bf16((perm_ref[...] >> shift) == here)
    in_row = dot_bf16(mine, before_in_row(LANES))
    ahead = dot_bf16(earlier, mine).astype(jnp.bfloat16)
    in_rows = dot_bf16(ahead, jnp.ones((LANES, LANES), jnp.bfloat16))
    place_ref[...] = owner_down * per_peer + (in_row + in_rows).astype(jnp.int32)


    def entries(g):
        at = pl.ds(pl.multiple_of(g * 8, 8), 8)
        series = perm_ref[at, :]
        key = jnp.where((series >> shift) == here, place_ref[at, :], -1)
        return key, (series & (ser_dev - 1)) + 1

    column = scatter(entries, rows // 8, SLOTS // LANES) - 1
    loads[3].wait()
    chunks = [x_ref[:, c * LANES : (c + 1) * LANES] for c in range(ser_dev // LANES)]
    stores = [
        pltpu.make_async_copy(send_ref.at[o], send_hbm.at[o], out_sems.at[o])
        for o in range(n_ser)
    ]
    for k in range(SLOTS // LANES):
        taken = take_columns(chunks, column[k : k + 1])
        first = k * LANES // per_peer
        if per_peer >= LANES:
            start = k * LANES % per_peer
            send_ref[first, :, start : start + LANES] = taken
            if start + LANES == per_peer:
                stores[first].start()
        else:
            for h in range(LANES // per_peer):
                send_ref[first + h] = taken[:, h * per_peer : (h + 1) * per_peer]
                stores[first + h].start()
    for store in stores:
        store.wait()


def eliminate(parts, size, whole):
    lane = iota((8, LANES), 1)
    sub = iota((8, LANES), 0)
    base = lane & (LANES - size)
    local = lane & (size - 1)
    parts = [list(part) for part in parts]
    downs = [[jnp.ones((8, LANES), jnp.float32)] * len(part) for part in parts]
    acrosses = [jnp.ones((8, LANES), jnp.float32) for _ in parts]
    tall = PANEL // 8
    count = PIVOTS
    for top in range(0, size, PANEL):
        first = top // 8
        inside = (local >= top) & (local < top + PANEL)
        panels = [part[first : first + tall] for part in parts]
        kept = [list(panel) for panel in panels]
        for j in range(top, top + PANEL, count):
            g, s = divmod(j - top, 8)
            columns = [base + (j + a) for a in range(count)]
            at = [local == j + a for a in range(count)]
            on = (local >= j) & (local < j + count)
            for p, panel in enumerate(panels):
                picked = [[lane_pick(piece, column) for column in columns] for piece in panel]
                corner = [
                    [
                        jnp.broadcast_to(picked[g][b][s + a : s + a + 1], (8, LANES))
                        for b in range(a + 1)
                    ]
                    for a in range(count)
                ]
                inv, low = [], [[None] * count for _ in range(count)]
                for k in range(count):
                    inv.append(1.0 / corner[k][k])
                    for a in range(k + 1, count):
                        low[a][k] = corner[a][k] * inv[k]
                    for a in range(k + 1, count):
                        for b in range(k + 1, a + 1):
                            corner[a][b] = corner[a][b] - low[a][k] * corner[b][k]
                rows, solved = [], [None] * count
                for a in range(count):
                    row = jnp.broadcast_to(panel[g][s + a : s + a + 1], (8, LANES))
                    row = jnp.where(on, jnp.where(at[a], 1.0, 0.0), row)
                    for b in range(a):
                        row = row - low[a][b] * rows[b]
                    rows.append(row)
                for a in reversed(range(count)):
                    row = rows[a] * inv[a]
                    for b in reversed(range(a + 1, count)):
                        row = row - low[b][a] * solved[b]
                    solved[a] = row
                for v in range(tall):
                    if v == g and count == 8:
                        new = solved[0]
                        for a in range(1, count):
                            new = jnp.where(sub == a, solved[a], new)
                        panel[v] = new
                        continue
                    new = jnp.where(on, 0.0, panel[v])
                    for a in reversed(range(count)):
                        new = new - picked[v][a] * solved[a]
                    if v == g:
                        for a in range(count):
                            new = jnp.where(sub == s + a, solved[a], new)
                    panel[v] = new
                if not whole:
                    if count < 8:
                        kept[p][g] = jnp.where(sub >= s + count, panel[g], kept[p][g])
                    kept[p][g + 1 :] = panel[g + 1 :]
                    for a in range(count):
                        here = sub == s + a
                        pivot = corner[a][a]
                        kept[p][g] = jnp.where(here, rows[a], kept[p][g])
                        downs[p][first + g] = jnp.where(here, pivot, downs[p][first + g])
                        acrosses[p] = jnp.where(at[a], pivot, acrosses[p])
        for p, part in enumerate(parts):
            others = [i for i in range(len(part)) if i >= first + tall or (whole and i < first)]
            if others:
                zero = jnp.zeros((8, LANES), jnp.float32)
                pieces = []
                for h in range(LANES // size):
                    half = base == h * size
                    for i in range(size // 8):
                        if first <= i < first + tall:
                            pieces.append(jnp.where(half, panels[p][i - first], 0.0))
                        else:
                            pieces.append(zero)
                change = dot_f32(
                    jnp.concatenate([part[i] for i in others], axis=0),
                    jnp.concatenate(pieces, axis=0),
                )
                for n, i in enumerate(others):
                    part[i] = jnp.where(inside, 0.0, part[i]) - change[n * 8 : n * 8 + 8]
            part[first : first + tall] = panels[p] if whole else kept[p]
    return parts, downs, acrosses


def slots_body(
    size_ref,
    owner_ref,
    perm_ref,
    place_ref,
    pick_ref,
    tile_of_ref,
    tile_ref,
    dest_ref,
    index_ref,
    *,
    n_ser,
    n_org,
    ser_dev,
):
    here = lax.axis_index("ser")
    part = lax.axis_index("org")
    n_sub = size_ref.shape[0]
    per_peer = SLOTS // n_ser
    share = SLOTS // n_org
    tiles = share // TILE
    shift = ser_dev.bit_length() - 1
    slot_rows = SLOTS // LANES
    wide = max(per_peer, LANES)

    def entries(g):
        at = pl.ds(pl.multiple_of(g * 8, 8), 8)
        series = perm_ref[at, :]
        return jnp.where((series >> shift) == here, series & (ser_dev - 1), -1), place_ref[at, :]

    dest_ref[...] = scatter(entries, perm_ref.shape[0] // 8, ser_dev // LANES)

    for t in range(OWNER_TILES):
        tile_ref[0, t] = jnp.int32(-1)
        tile_ref[1, t] = jnp.int32(0)
        tile_ref[2, t] = jnp.int32(0)
    at = jnp.int32(0)
    first = jnp.int32(0)
    for k in range(n_sub):
        count = size_ref[k] >> 8
        held = jnp.where(owner_ref[k] == here, count, 0)

        def put(i, carry, at=at, first=first, held=held):
            tile_ref[0, at + i] = first + i
            tile_ref[1, at + i] = at
            tile_ref[2, at + i] = at + held
            return carry

        lax.fori_loop(0, held, put, 0)
        at = at + held
        first = first + count

    pieces = []
    for t in range(OWNER_TILES):
        place = tile_ref[0, t]
        rows = perm_ref[pl.ds(jnp.maximum(place, 0) * ROWS, ROWS), :]
        pieces.append(jnp.where(place >= 0, rows, -1))
    source = jnp.concatenate(pieces, axis=0) >> shift
    from_peer = jnp.concatenate([as_bf16(source == d) for d in range(n_ser)], axis=0)
    in_row = dot_bf16(from_peer, before_in_row(LANES))
    row_total = dot_bf16(from_peer, jnp.ones((LANES, wide), jnp.bfloat16)).astype(jnp.bfloat16)
    span = n_ser * slot_rows
    left, right = iota((span, span), 0), iota((span, span), 1)
    ahead = as_bf16((left // slot_rows == right // slot_rows) & (right < left))
    base = dot_bf16(ahead, row_total)[:, :LANES]
    rank = jnp.zeros((slot_rows, LANES), jnp.float32)
    for d in range(n_ser):
        rows = slice(d * slot_rows, (d + 1) * slot_rows)
        rank = jnp.where(source == d, in_row[rows] + base[rows], rank)
    index_ref[...] = jnp.where(source >= 0, source * per_peer + rank.astype(jnp.int32), -1)
    left, right = iota((OWNER_TILES * n_ser, span), 0), iota((OWNER_TILES * n_ser, span), 1)
    through = as_bf16(
        (left % n_ser == right // slot_rows)
        & (right % slot_rows < ROWS * (left // n_ser) + ROWS)
    )
    ends = dot_bf16(through, row_total).astype(jnp.int32)[:, :per_peer]
    tile_of = jnp.zeros((n_ser, per_peer), jnp.int32)
    for t in range(OWNER_TILES):
        tile_of += (iota((n_ser, per_peer), 1) >= ends[t * n_ser : (t + 1) * n_ser]).astype(
            jnp.int32
        )
    tile_of = jnp.concatenate([tile_of[d : d + 1] for d in range(n_ser)], axis=1)
    tile_of_ref[...] = tile_of

    for i in range(share // LANES):
        row = index_ref[pl.ds(part * (tiles * ROWS) + i, 1), :]
        pick_ref[:, i * LANES : (i + 1) * LANES] = as_bf16(iota((SLOTS, LANES), 0) == row)


def owner_body(*refs, n_ser, n_org, flips):
    recv_refs = refs[:n_org]
    pick_ref, tile_of_ref, tile_ref, back_ref, log_ref, all_ref, inverse_ref = refs[n_org:]
    part = lax.axis_index("org")
    t_dev = recv_refs[0].shape[1]
    anchors = t_dev * n_org
    per_peer = SLOTS // n_ser
    share = SLOTS // n_org
    tiles = share // TILE

    for flip, part_ref in zip(flips, recv_refs):
        row = pl.multiple_of((part ^ flip) * t_dev, t_dev)
        for d in range(n_ser):
            all_ref[pl.ds(row, t_dev), d * per_peer : (d + 1) * per_peer] = part_ref[d]

    tile_of = tile_of_ref[...]

    block = all_ref[...]
    spread = jnp.sum(block * block, axis=0, keepdims=True) * (1.0 / anchors)
    scaled = block * jnp.where(spread > 0, lax.rsqrt(spread), 0.0)
    own = spread / (spread + epsilon)
    fourth = jnp.sum(jnp.square(scaled * scaled), axis=0, keepdims=True) * (1.0 / anchors)
    in_tree, ahead_of, filled = [], [], []
    for u in range(tiles):
        t = part * tiles + u
        low, high = tile_ref[1, t], tile_ref[2, t]
        filled.append(tile_ref[0, t] >= 0)
        in_tree.append((tile_of >= low) & (tile_of < high))
        ahead_of.append((tile_of >= low) & (tile_of < t))
    terms = split_three(scaled)
    weighted = split_three(scaled * own)
    products = dot_bf16(
        jnp.concatenate(
            [weighted * as_bf16(mask) for mask in in_tree]
            + [terms * as_bf16(mask) for mask in ahead_of],
            axis=0,
        ),
        terms,
        NT,
    )
    grams = []
    for u in range(2 * tiles):
        piece = join_three(products[u * 3 * anchors : (u + 1) * 3 * anchors])
        grams.append(
            piece[:, 2 * anchors :] + piece[:, anchors : 2 * anchors] + piece[:, :anchors]
        )
    unit = iota((anchors, anchors), 0) == iota((anchors, anchors), 1)
    shrink = []
    for u in range(tiles):
        dual = grams[u] * (1.0 / anchors)
        own_square = jnp.where(in_tree[u], own * own, 0.0)
        square = dual * dual
        total = lambda value: jnp.sum(
            jnp.sum(value, axis=0, keepdims=True), axis=1, keepdims=True
        )
        lower = total(square) - total(own_square)
        upper = total(jnp.where(unit, square, 0.0)) * anchors - total(own_square * fourth)
        upper = (upper - lower) / (anchors - 1)
        shrink.append(jnp.where(filled[u], jnp.minimum(upper / jnp.where(filled[u], lower, 1.0), 1.0), 1.0))

    levels = split_three(jnp.broadcast_to(spread, (16, SLOTS)))
    found = dot_bf16(jnp.concatenate([terms, levels], axis=0), pick_ref[...])
    mine = join_three(found[: 3 * anchors])
    my_spread = join_three(found[3 * anchors :])[:1]
    mine_down = mine.T

    per_tile = TILE // BLOCK
    blocks = share // BLOCK
    side = LANES // anchors
    rows_of = lambda b: slice(b * BLOCK, (b + 1) * BLOCK)
    for u in range(tiles):
        prior = grams[tiles + u]
        gain = (1.0 - shrink[u]) * (1.0 / anchors)
        for v in range(per_tile):
            b = u * per_tile + v
            inverse_ref[b // side, :, (b % side) * anchors : (b % side + 1) * anchors] = (
                jnp.where(unit, shrink[u], 0.0) + gain * prior
            )
            if v < per_tile - 1:
                piece = mine[:, rows_of(b)]
                prior = prior + dot_f32(piece, piece, NT)

    inverses, _, _ = eliminate(
        [
            [inverse_ref[p, i * 8 : (i + 1) * 8, :] for i in range(anchors // 8)]
            for p in range(blocks // side)
        ],
        anchors,
        whole=True,
    )
    inverses = [jnp.concatenate(rows, axis=0) for rows in inverses]

    diagonal = iota((BLOCK, BLOCK), 0) == iota((BLOCK, BLOCK), 1)
    solved, weights = [], []
    for b in range(blocks):
        gain = (1.0 - shrink[b // per_tile]) * (1.0 / anchors)
        inverse = inverses[b // side][:, (b % side) * anchors : (b % side + 1) * anchors]
        solved.append(dot_f32(inverse, mine[:, rows_of(b)]))
        weights.append(
            jnp.where(diagonal, 1.0, 0.0) + gain * dot_f32(mine_down[rows_of(b)], solved[b])
        )
    pairs = [jnp.concatenate(weights[b : b + 2], axis=1) for b in range(0, blocks, 2)]
    lowers, downs, acrosses = eliminate(
        [[pair[i * 8 : (i + 1) * 8] for i in range(BLOCK // 8)] for pair in pairs],
        BLOCK,
        whole=False,
    )
    keep = iota((BLOCK, LANES), 0) >= (iota((BLOCK, LANES), 1) & (BLOCK - 1))
    done, logs = [], []
    for p in range(blocks // 2):
        lower = jnp.concatenate(
            [row * lax.rsqrt(pivot) for row, pivot in zip(lowers[p], downs[p])], axis=0
        )
        lower = jnp.where(keep, lower, 0.0)
        for h in range(2):
            b = 2 * p + h
            u = b // per_tile
            half = slice(h * BLOCK, (h + 1) * BLOCK)
            done.append(dot_f32(solved[b], lower[:, half], NT) * jnp.sqrt(shrink[u]))
            level = acrosses[p][:1, half] * my_spread[:, rows_of(b)] * shrink[u]
            logs.append(jnp.where(filled[u], 0.5 * jnp.log(level), 0.0))
    log_ref[...] = jnp.concatenate(logs, axis=1)
    terms = split_three(jnp.concatenate(done, axis=1))

    for d in range(n_ser):
        columns = join_three(
            dot_bf16(terms, pick_ref[d * per_peer : (d + 1) * per_peer, :], NT)
        )
        for r in range(n_org):
            back_ref[d * n_org + r] = columns[r * t_dev : (r + 1) * t_dev]


def home_body(back_ref, dest_ref, out_ref, *, n_ser, n_org):
    per_peer = back_ref.shape[2]
    pieces = []
    for o in range(n_ser):
        piece = back_ref[o * n_org]
        for q in range(1, n_org):
            piece = piece + back_ref[o * n_org + q]
        pieces.append(piece)
    whole = jnp.concatenate(pieces, axis=1)
    chunks = [whole[:, c * LANES : (c + 1) * LANES] for c in range(SLOTS // LANES)]
    for h in range(dest_ref.shape[0]):
        out_ref[:, h * LANES : (h + 1) * LANES] = take_columns(chunks, dest_ref[h : h + 1, :])


def per_device(residual, sub_size, sub_owner, series_perm):
    n_ser = lax.axis_size("ser")
    n_org = lax.axis_size("org")
    t_dev, ser_dev = residual.shape
    anchors = t_dev * n_org
    per_peer = SLOTS // n_ser
    share = SLOTS // n_org
    blocks = share // BLOCK
    side = LANES // anchors
    perm = series_perm.reshape(-1, LANES)
    to_hbm = lambda value: pltpu.with_memory_space_constraint(value, pltpu.HBM)
    vmem = pl.BlockSpec(memory_space=pltpu.VMEM)
    smem = pl.BlockSpec(memory_space=pltpu.SMEM)
    hbm = pl.BlockSpec(memory_space=pltpu.HBM)
    params = pltpu.CompilerParams(vmem_limit_bytes=48 * 1024 * 1024)
    blocks_shape = jax.ShapeDtypeStruct((n_ser * n_org, t_dev, per_peer), jnp.float32)

    send, place = pl.pallas_call(
        functools.partial(pack_body, n_ser=n_ser, n_org=n_org),
        out_shape=(jax.ShapeDtypeStruct((n_ser, t_dev, per_peer), jnp.float32), jax.ShapeDtypeStruct(perm.shape, jnp.int32)),
        in_specs=[hbm, hbm, hbm, hbm],
        out_specs=(hbm, vmem),
        scratch_shapes=[
            pltpu.SMEM(sub_size.shape, jnp.int32),
            pltpu.SMEM(sub_owner.shape, jnp.int32),
            pltpu.VMEM(residual.shape, jnp.float32),
            pltpu.VMEM(perm.shape, jnp.int32),
            pltpu.VMEM((n_ser, t_dev, per_peer), jnp.float32),
            pltpu.SemaphoreType.DMA((4,)),
            pltpu.SemaphoreType.DMA((n_ser,)),
        ],
        compiler_params=params,
        name="pack",
    )(to_hbm(sub_size), to_hbm(sub_owner), to_hbm(residual), to_hbm(perm))
    recv = lax.all_to_all(send, "ser", split_axis=0, concat_axis=0, tiled=True)
    pick, tile_of, tile, dest = pl.pallas_call(
        functools.partial(slots_body, n_ser=n_ser, n_org=n_org, ser_dev=ser_dev),
        out_shape=(
            jax.ShapeDtypeStruct((SLOTS, share), jnp.bfloat16),
            jax.ShapeDtypeStruct((1, SLOTS), jnp.int32),
            jax.ShapeDtypeStruct((3, OWNER_TILES), jnp.int32),
            jax.ShapeDtypeStruct((ser_dev // LANES, LANES), jnp.int32),
        ),
        in_specs=[smem, smem, vmem, vmem],
        out_specs=(vmem, vmem, smem, vmem),
        scratch_shapes=[pltpu.VMEM((SLOTS // LANES, LANES), jnp.int32)],
        compiler_params=params,
        cost_estimate=pl.CostEstimate(
            flops=4_000_000_000, bytes_accessed=4_000_000, transcendentals=0
        ),
        name="slots",
    )(sub_size, sub_owner, perm, place)
    recv, pick, tile_of, tile, dest = lax.optimization_barrier(
        (recv, pick, tile_of, tile, dest)
    )
    received, flips, bit = [recv], [0], n_org // 2
    while bit:
        swap = [(i, i ^ bit) for i in range(n_org)]
        received = received + [lax.ppermute(part, "org", swap) for part in received]
        flips = flips + [flip ^ bit for flip in flips]
        bit //= 2
    back, log_part = pl.pallas_call(
        functools.partial(owner_body, n_ser=n_ser, n_org=n_org, flips=flips),
        out_shape=(blocks_shape, jax.ShapeDtypeStruct((1, share), jnp.float32)),
        in_specs=[vmem] * n_org + [vmem, vmem, smem],
        out_specs=(vmem, vmem),
        scratch_shapes=[
            pltpu.VMEM((anchors, SLOTS), jnp.float32),
            pltpu.VMEM((blocks // side, anchors, LANES), jnp.float32),
        ],
        compiler_params=params,
        name="owner",
    )(*received, pick, tile_of, tile)
    returned = lax.all_to_all(back, ("ser", "org"), split_axis=0, concat_axis=0, tiled=True)
    whitened = pl.pallas_call(
        functools.partial(home_body, n_ser=n_ser, n_org=n_org),
        out_shape=jax.ShapeDtypeStruct((t_dev, ser_dev), jnp.float32),
        in_specs=[vmem, vmem],
        out_specs=vmem,
        compiler_params=params,
        name="home",
    )(returned, dest)
    return (whitened, log_part)


def solution(mesh):
    in_specs = (P("org", "ser"), P(), P(), P())
    out_specs = (P("org", "ser"), P("ser", "org"))
    return jax.shard_map(
        per_device, mesh=mesh, in_specs=in_specs, out_specs=out_specs, check_vma=False
    )
```
